128 devices in a mesh: gr: 16 (over z, y_hi, core), gc: 8 (over x, y_lo).
Axes of the slice: x: 4, y: 4 (y_hi: 2, y_lo: 2; y = y_hi * 2 + y_lo), z: 4, core: 2. Of those that a mesh axis runs over, the one named last changes fastest.
Arguments:
- right_sides: float32 [131072, 1024], P('gr', 'gc'), may hold values from -6 to 6
- factor_panel: bfloat16 [3, 131072, 1024], P(None, ('gr', 'gc')), may hold values from -0.1875 to 0.1875
- diag_inverse: bfloat16 [3, 1024, 1024], replicated, as said below
- block_ids: int32 [128], replicated, may hold values from 0 to 127, each once
- step_blocks: int32 [3], replicated, may hold values from 0 to 33, as said below
Outputs:
- solved_rhs: float32 [131072, 1024], P('gr', 'gc')
The draws below stay inside these ranges and needn't reach their ends.
Inputs may be any that keep to these rules, and one draw needn't show every extreme that they name: `block_ids`: each number appears once. `step_blocks`: 3 distinct rising block numbers, the first 0 and the last 33. `diag_inverse`: lower triangular with a positive diagonal.
All inputs are finite; a program needn't handle non-finite values.
Results may differ from the reference program's by a relative error of at most 0.0059.
Values may be sent and summed in bfloat16 or wider, within the bound.
A program may use at most 128 MiB of HBM per device.

```python
import jax
import jax.numpy as jnp
from jax import lax

NB = 1024
R = 1024
STEPS = 3
NBLK = 128
N = 131072


def draw_diag_inverse(key, part):
    key = jax.random.fold_in(key, 11)
    first_key, second_key = jax.random.split(key)
    lower = jax.random.normal(first_key, (STEPS, NB, NB), jnp.float32) * NB ** (-0.5)
    diagonal = jax.random.uniform(second_key, (STEPS, NB), jnp.float32, 0.6, 1.5)
    rows_index = jnp.arange(NB)[:, None]
    cols_index = jnp.arange(NB)[None, :]
    strict = (rows_index > cols_index)[None, :, :]
    ident = (rows_index == cols_index)[None, :, :]
    result = jnp.where(strict, lower, 0.0) + jnp.where(ident, diagonal[:, :, None], 0.0)
    return result.astype(jnp.bfloat16)


def draw_step_blocks(key, part):
    key = jax.random.fold_in(key, 7)
    last_block = NBLK // 4 + STEPS - 2
    inner = jax.random.permutation(key, jnp.arange(1, last_block, dtype=jnp.int32))
    middle = jnp.sort(inner[:STEPS - 2])
    first = jnp.zeros((1,), jnp.int32)
    final = jnp.full((1,), last_block, jnp.int32)
    return jnp.concatenate([first, middle, final]).astype(jnp.int32)


def block_scale(rng, shape, shards, low, high):
    def one(dim, blocks):
        draws = jax.random.uniform(jax.random.fold_in(jax.random.fold_in(rng, 6), dim), (blocks,), jnp.float32, low / len(shards), high / len(shards))
        return jnp.repeat(jnp.exp(draws), shape[dim] // blocks).reshape((-1,) + (1,) * (len(shape) - dim - 1))

    factor_of = one(*shards[0])
    for cut in shards[1:]:
        factor_of = factor_of * one(*cut)
    return factor_of


def gaussian(stream_key, extent, width, most, shards=(), kind=jnp.bfloat16):
    entries = jax.random.normal(stream_key, extent, jnp.float32) * width
    if len(shards) > 0:
        entries = block_scale(stream_key, extent, shards, -0.22, 0.18) * entries
    return jnp.clip(entries, min=-most, max=most).astype(kind)


def setup_inputs(seed: int = 0) -> dict:
    seeds = jax.random.split(jax.random.key(seed), 6)
    right_sides = gaussian(seeds[0], (N, R), 1.0, 6.0, ((0, 16), (1, 8)), jnp.float32)
    factor_panel = gaussian(seeds[1], (STEPS, N, NB), NB ** -0.5, 0.1875, ((1, 128),))
    diag_inverse = draw_diag_inverse(jax.random.fold_in(seeds[5], 71), 0)
    block_ids = jax.random.permutation(seeds[3], NBLK).astype(jnp.int32)
    step_blocks = draw_step_blocks(jax.random.fold_in(seeds[5], 71), 0)
    return {"right_sides": right_sides, "factor_panel": factor_panel, "diag_inverse": diag_inverse, "block_ids": block_ids, "step_blocks": step_blocks}


def reference(right_sides, factor_panel, diag_inverse, block_ids, step_blocks):
    numbering = jnp.arange(NBLK, dtype=jnp.int32)
    current = right_sides
    solved = []
    for step in range(STEPS):
        block_no = step_blocks[step]
        position = jnp.sum(jnp.where(block_ids == block_no, numbering, 0)).astype(jnp.int32)
        target = lax.dynamic_slice_in_dim(current, position * NB, NB, 0)
        y_block = jnp.dot(diag_inverse[step].astype(jnp.float32), target, precision=lax.Precision.HIGHEST)
        solved.append((position, y_block))
        contrib = jnp.dot(factor_panel[step], y_block.astype(jnp.bfloat16), preferred_element_type=jnp.float32).astype(jnp.bfloat16)
        pending = block_ids > block_no
        shaped = current.reshape(NBLK, NB, R)
        shaped = shaped - jnp.where(pending[:, None, None], contrib.reshape(NBLK, NB, R).astype(current.dtype), 0.0)
        current = shaped.reshape(N, R)
    for position, y_block in solved:
        current = lax.dynamic_update_slice_in_dim(current, y_block, position * NB, 0)
    return current
```

```python
import jax
import jax.numpy as jnp
from jax import lax
from jax.experimental import pallas as pl
from jax.experimental.pallas import tpu as pltpu
from jax.sharding import PartitionSpec as P

MESH = pl.DeviceIdType.MESH
F32 = jnp.float32
BF16 = jnp.bfloat16
NB = 1024
HALF = 512
COLS = 128
ROW_PEERS = ((0, 1), (1, 0), (3, 0), (1, 1), (3, 1), (2, 0), (2, 1))
INVERSE = tuple(ROW_PEERS.index(((4 - dx) % 4, flip)) for dx, flip in ROW_PEERS)
ORDERS = ((0, 1, 2), (1, 2, 0), (2, 0, 1))


def dot(a, b):
    return jnp.dot(a, b, preferred_element_type=F32)


def kernel(
    flags, rhs_ref, panel_ref, diag_ref, out_ref,
    rhs, panel, diag, fin, w, w2, r1, r2, r3,
    thl, a0, stage, a_in, a_half, a_z, a_piece, a_y, afull,
    yf, ysol, g0_out, g0_in, g1_out, g1_in, acc, c_out, c_in,
    load_sem, out_sem, fin_s, fin_r, sel_s, sel_r, a_s, a_r, y_s, y_r, fw_s, fw_r, g_s, g_r, c_s, c_r,
):
    gr, gc = lax.axis_index("gr"), lax.axis_index("gc")
    z, y_hi, core = gr // 4, (gr // 2) % 2, gr % 2
    x, y_lo = gc // 2, gc % 2
    y = y_hi * 2 + y_lo
    other = 1 - core
    here = (x, y, z)

    def device(at, c):
        return (at[2] * 4 + (at[1] // 2) * 2 + c, at[0] * 2 + at[1] % 2)

    def along(axis, step):
        at = list(here)
        at[axis] = (at[axis] + step) % 4
        return device(at, core)

    def row_peer(i, sign):
        dx, flip = ROW_PEERS[i]
        return ((x + sign * dx + 4) % 4) * 2 + (y_lo + flip) % 2

    def send(src, dst, s, r, to):
        copy = pltpu.make_async_remote_copy(
            src_ref=src, dst_ref=dst, send_sem=s, recv_sem=r, device_id=to, device_id_type=MESH
        )
        copy.start()
        return copy

    def local(src, dst, sem):
        copy = pltpu.make_async_copy(src, dst, sem)
        copy.start()
        return copy

    partner = (gr + 1 - 2 * core, gc)
    mine = pl.ds(pl.multiple_of(core * HALF, HALF), HALF)
    theirs = pl.ds(pl.multiple_of(other * HALF, HALF), HALF)

    load_f = [local(panel_ref.at[t], panel.at[t], load_sem.at[t]) for t in range(2)]
    load_rhs = local(rhs_ref, rhs, load_sem.at[3])
    load_d = local(diag_ref, diag, load_sem.at[4])
    load_f.append(local(panel_ref.at[2], panel.at[2], load_sem.at[2]))

    peers = [along(axis, step) for axis in range(3) for step in (1, 2, 3)]
    peers += [(gr, row_peer(i, 1)) for i in (3, 4, 6)] + [partner]
    barrier = pltpu.get_barrier_semaphore()
    for peer in peers:
        pl.semaphore_signal(barrier, inc=1, device_id=peer, device_id_type=MESH)
    pl.semaphore_wait(barrier, len(peers))

    fin_copies = []
    for t in range(2):
        for h in range(2):
            i = t * 2 + h
            fin_copies.append(
                send(
                    panel_ref.at[t, theirs, pl.ds(h * HALF, HALF)],
                    fin.at[t, pl.ds(h * HALF, HALF)],
                    fin_s.at[i], fin_r.at[i], partner,
                )
            )

    def flag(row):
        return flags[row:row + 1, :]

    def build(slot, t, row):
        def mask(r):
            tile = jnp.broadcast_to(flag(r), (128, COLS)).astype(BF16)
            return jnp.concatenate([tile] * (HALF // COLS), axis=1)

        own, oth = mask(row), mask(row + 1)

        def chunk(i, carry):
            rows = pl.ds(pl.multiple_of(core * HALF + i * 128, 128), 128)
            for h in range(2):
                to = pl.ds(pl.multiple_of(h * HALF + i * 128, 128), 128)
                w[slot, to] = panel[t, rows, pl.ds(h * HALF, HALF)] * own + fin[t, to] * oth
            return carry

        lax.fori_loop(0, 4, chunk, 0)

    bases = []
    for slot in range(3):
        v = [here[a] for a in ORDERS[slot]]
        bases.append((v, (0, v[0] * 256, v[0] * 256 + v[1] * 64)))
    sizes = (256, 64, 16)

    def sem_at(slot, stage_no, step):
        return (slot * 6 + stage_no) * 3 + step - 1

    def scatter(slot, st):
        v, base = bases[slot]
        size = sizes[st]
        buf = (r1, r2, r3)[st]
        out = []
        for step in (1, 2, 3):
            rows = pl.ds(pl.multiple_of(base[st] + ((v[st] + step) % 4) * size, size), size)
            i = sem_at(slot, st, step)
            out.append(
                send(
                    w.at[slot, rows], buf.at[slot, step - 1], sel_s.at[i], sel_r.at[i],
                    along(ORDERS[slot][st], step),
                )
            )
        return out

    def total(slot, st, copies):
        v, base = bases[slot]
        size = sizes[st]
        buf = (r1, r2, r3)[st]
        for copy in copies:
            copy.wait()
        start = base[st] + v[st] * size
        span = min(size, 64)

        def chunk(i, carry):
            rows = pl.ds(pl.multiple_of(start + i * span, span), span)
            part = pl.ds(pl.multiple_of(i * span, span), span)
            value = w[slot, rows] + buf[slot, 0, part] + (buf[slot, 1, part] + buf[slot, 2, part])
            if st == 2:
                w2[slot, rows] = value
            else:
                w[slot, rows] = value
            return carry

        lax.fori_loop(0, size // span, chunk, 0)

    def gather(slot, st):
        v, base = bases[slot]
        size = sizes[st]
        rows = pl.ds(pl.multiple_of(base[st] + v[st] * size, size), size)
        out = []
        for step in (1, 2, 3):
            i = sem_at(slot, 5 - st, step)
            out.append(
                send(
                    w2.at[slot, rows], w2.at[slot, rows], sel_s.at[i], sel_r.at[i],
                    along(ORDERS[slot][st], step),
                )
            )
        return out

    def finish(copies):
        for copy in copies:
            copy.wait()

    for copy in load_f[:2]:
        copy.wait()
    finish(fin_copies[:2])
    run = [None] * 3
    build(0, 0, 24)
    run[0] = scatter(0, 0)
    build(1, 0, 26)
    run[1] = scatter(1, 0)
    finish(fin_copies[2:])
    build(2, 1, 26)
    run[2] = scatter(2, 0)

    load_rhs.wait()
    load_d.wait()
    for t in range(3):

        def split(i, carry, t=t):
            rows = pl.ds(pl.multiple_of(i * 128, 128), 128)
            value = jnp.zeros((128, COLS), F32)
            for j in range(8):
                block = rhs[pl.ds(pl.multiple_of(j * NB + i * 128, 128), 128), :]
                value = jnp.where(flag(t * 8 + j) > 0.5, block, value)
            high = value.astype(BF16)
            thl[rows, pl.ds(0, COLS)] = high
            thl[rows, pl.ds(COLS, COLS)] = (value - high.astype(F32)).astype(BF16)
            return carry

        lax.fori_loop(0, 8, split, 0)

        def solve(i, carry, t=t):
            rows = pl.ds(pl.multiple_of(i * 256, 256), 256)
            both = dot(diag[t, rows], thl[...])
            value = both[:, :COLS] + both[:, COLS:]
            high = value.astype(BF16)
            if t == 0:
                a0[rows] = value
                stage[0, rows] = high
            else:
                stage[2 * t - 1, rows] = high
                stage[2 * t, rows] = (value - high.astype(F32)).astype(BF16)
            return carry

        lax.fori_loop(0, 4, solve, 0)

    a_copy = send(stage.at[:, theirs], a_in, a_s.at[0], a_r.at[0], partner)
    a_copy.wait()
    for t in range(5):
        a_half[t] = stage[t, mine] + a_in[t]
    z_rows = [pl.ds(pl.multiple_of(((z + step) % 4) * 128, 128), 128) for step in range(4)]
    z_copies = [
        send(a_half.at[:, z_rows[step]], a_z.at[step - 1], a_s.at[step], a_r.at[step], along(2, step))
        for step in (1, 2, 3)
    ]

    for slot in range(3):
        total(slot, 0, run[slot])
        run[slot] = scatter(slot, 1)

    finish(z_copies)
    for t in range(5):
        a_piece[t] = a_half[t, z_rows[0]] + a_z[0, t] + (a_z[1, t] + a_z[2, t])
    y_copy = send(a_piece, a_y, a_s.at[4], a_r.at[4], along(1, 2))

    for slot in range(3):
        total(slot, 1, run[slot])
        run[slot] = scatter(slot, 2)

    y_copy.wait()
    piece = pl.ds(pl.multiple_of(core * HALF + z * 128, 128), 128)
    for t in range(5):
        afull[t, piece] = a_piece[t] + a_y[t]
    z_copies = [
        send(afull.at[:, piece], afull.at[:, piece], a_s.at[4 + step], a_r.at[4 + step], along(2, step))
        for step in (1, 2, 3)
    ]

    for slot in range(3):
        total(slot, 2, run[slot])
        run[slot] = gather(slot, 2)

    finish(z_copies)
    a_copy = send(afull.at[:, mine], afull.at[:, mine], a_s.at[8], a_r.at[8], partner)

    def publish(t, src):
        return [
            send(src, yf.at[t, gc, mine], y_s.at[t * 7 + i], y_r.at[t * 7 + i], (gr, row_peer(i, 1)))
            for i in range(7)
        ]

    def forward(t, i, copy):
        copy.wait()
        block = yf.at[t, row_peer(i, -1), mine]
        j = t * 7 + i
        return send(block, block, fw_s.at[j], fw_r.at[j], partner)

    y_copies = publish(0, afull.at[0, mine])

    for slot in range(3):
        finish(run[slot])
        run[slot] = gather(slot, 1)
    a_copy.wait()
    yf[0, gc] = afull[0]
    for slot in range(3):
        finish(run[slot])
        run[slot] = gather(slot, 0)

    forwards = [forward(0, i, y_copies[i]) for i in range(7)]
    finish(forwards)

    def contribute(t, first):
        keep = jnp.concatenate([flag(28 + t)] * 2, axis=1) > 0.5

        def pair(i, carry):
            right = jnp.concatenate([yf[t, 2 * i], yf[t, 2 * i + 1]], axis=1)

            def tile(m, inner):
                rows = pl.ds(pl.multiple_of(m * 256, 256), 256)
                value = dot(panel[t, rows], right)
                value = jnp.where(keep, value, jnp.zeros_like(value))
                for e in range(2):
                    part = value[:, e * COLS:(e + 1) * COLS]
                    acc[2 * i + e, rows] = part if first else acc[2 * i + e, rows] + part
                return inner

            lax.fori_loop(0, 4, tile, 0)
            return carry

        lax.fori_loop(0, 4, pair, 0)

    contribute(0, True)

    def product(slot, t, i):
        rows = pl.ds(pl.multiple_of(i * 256, 256), 256)
        low = pl.ds(pl.multiple_of(HALF + i * 256, 256), 256)
        return dot(w2[slot, rows], yf[t, gc, pl.ds(0, HALF)]) + dot(
            w2[slot, low], yf[t, gc, pl.ds(HALF, HALF)]
        )

    def exchange(n, g_out, g_in):
        copy = send(g_out.at[mine], g_in.at[mine], g_s.at[n], g_r.at[n], partner)
        copy.wait()

    def next_y(t, g_in):
        def tile(i, carry):
            rows = pl.ds(pl.multiple_of(i * 256, 256), 256)
            value = afull[2 * t - 1, rows].astype(F32) + afull[2 * t, rows].astype(F32)
            change = dot(diag[t, rows], g_in[...])
            for e in range(t):
                value = value - change[:, e * COLS:(e + 1) * COLS]
            ysol[t - 1, rows] = value
            yf[t, gc, rows] = value.astype(BF16)
            return carry

        lax.fori_loop(0, 4, tile, 0)

    def store_g(g_out, g_in, i, e, value):
        rows = pl.ds(pl.multiple_of(core * HALF + i * 256, 256), 256)
        short = value.astype(BF16)
        g_out[rows, pl.ds(e * COLS, COLS)] = short
        g_in[rows, pl.ds(e * COLS, COLS)] = short

    finish(run[0])
    for i in range(2):
        store_g(g0_out, g0_in, i, 0, product(0, 0, i))
    exchange(0, g0_out, g0_in)
    next_y(1, g0_in)
    y_copies = publish(1, yf.at[1, gc, mine])
    finish(run[1])
    finish(run[2])
    for i in range(2):
        store_g(g1_out, g1_in, i, 0, product(1, 0, i))
        store_g(g1_out, g1_in, i, 1, product(2, 1, i))
    exchange(1, g1_out, g1_in)
    next_y(2, g1_in)
    y2_copies = publish(2, yf.at[2, gc, mine])

    forwards = [forward(1, i, y_copies[i]) for i in range(7)]
    finish(forwards)
    contribute(1, False)

    load_f[2].wait()
    keep2 = flag(30) > 0.5

    def last(col, put):
        def tile(m, inner):
            rows = pl.ds(pl.multiple_of(m * 256, 256), 256)
            value = dot(panel[2, rows], yf[2, col])
            put(rows, (acc[col, rows] + jnp.where(keep2, value, jnp.zeros_like(value))).astype(BF16))
            return inner

        lax.fori_loop(0, 4, tile, 0)

    def put_own(rows, value):
        c_in[gc, rows] = value

    last(gc, put_own)
    c_copies = [None] * 7
    ahead = forward(2, 0, y2_copies[0])
    for i in range(7):
        arrived = ahead
        if i < 6:
            ahead = forward(2, i + 1, y2_copies[i + 1])
        arrived.wait()
        to = INVERSE[i]
        col = row_peer(i, -1)

        def put(rows, value, to=to):
            c_out[to, rows] = value

        last(col, put)
        c_copies[to] = send(c_out.at[to], c_in.at[gc], c_s.at[to], c_r.at[to], (gr, col))

    def settle(j):
        def tile(m, inner):
            rows = pl.ds(pl.multiple_of(j * NB + m * 256, 256), 256)
            part = pl.ds(pl.multiple_of(m * 256, 256), 256)
            value = rhs[rows, :] - c_in[j, part].astype(F32)
            for t, solved in enumerate((a0[part], ysol[0, part], ysol[1, part])):
                value = jnp.where(flags[pl.ds(t * 8 + j, 1), :] > 0.5, solved, value)
            rhs[rows, :] = value
            return inner

        lax.fori_loop(0, 4, tile, 0)
        rows = pl.ds(pl.multiple_of(j * NB, NB), NB)
        return rows

    stores = []
    rows = settle(gc)
    stores.append(local(rhs.at[rows], out_ref.at[rows], out_sem.at[7]))
    for i in range(7):
        c_copies[i].wait()
        rows = settle(row_peer(i, -1))
        stores.append(local(rhs.at[rows], out_ref.at[rows], out_sem.at[i]))
    finish(stores)


def shards(right_sides, factor_panel, diag_inverse, block_ids, step_blocks):
    gr, gc = lax.axis_index("gr"), lax.axis_index("gc")
    numbering = jnp.arange(128, dtype=jnp.int32)
    hit = block_ids[None, :] == step_blocks[:, None]
    place = jnp.sum(jnp.where(hit, numbering[None, :], 0), axis=1)
    own = place // 8 == gr
    inside = place % 8
    block = gr * 8 + gc
    beside = (gr + 1 - 2 * (gr % 2)) * 8 + gc
    my_id = jnp.sum(jnp.where(numbering == block, block_ids, 0))
    later = my_id > step_blocks
    chosen = own[:, None] & (inside[:, None] == numbering[None, :8])
    scalars = jnp.concatenate(
        [
            chosen.reshape(24),
            jnp.stack([place[1] == block, place[1] == beside, place[2] == block, place[2] == beside]),
            later,
            jnp.zeros((1,), bool),
        ]
    )
    flags = jnp.broadcast_to(scalars.astype(F32)[:, None], (32, COLS))
    dma = pltpu.SemaphoreType.DMA
    vm = pltpu.VMEM
    return pl.pallas_call(
        kernel,
        out_shape=jax.ShapeDtypeStruct((8 * NB, COLS), F32),
        in_specs=[pl.BlockSpec(memory_space=pltpu.VMEM)] + [pl.BlockSpec(memory_space=pl.ANY)] * 3,
        out_specs=pl.BlockSpec(memory_space=pl.ANY),
        scratch_shapes=[
            vm((8 * NB, COLS), F32),
            vm((3, NB, NB), BF16),
            vm((3, NB, NB), BF16),
            vm((2, NB, HALF), BF16),
            vm((3, NB, HALF), BF16),
            vm((3, NB, HALF), BF16),
            vm((3, 3, 256, HALF), BF16),
            vm((3, 3, 64, HALF), BF16),
            vm((3, 3, 16, HALF), BF16),
            vm((NB, 2 * COLS), BF16),
            vm((NB, COLS), F32),
            vm((5, NB, COLS), BF16),
            vm((5, HALF, COLS), BF16),
            vm((5, HALF, COLS), BF16),
            vm((3, 5, 128, COLS), BF16),
            vm((5, 128, COLS), BF16),
            vm((5, 128, COLS), BF16),
            vm((5, NB, COLS), BF16),
            vm((3, 8, NB, COLS), BF16),
            vm((2, NB, COLS), F32),
            vm((NB, COLS), BF16),
            vm((NB, COLS), BF16),
            vm((NB, 2 * COLS), BF16),
            vm((NB, 2 * COLS), BF16),
            vm((8, NB, COLS), F32),
            vm((7, NB, COLS), BF16),
            vm((8, NB, COLS), BF16),
            dma((5,)), dma((8,)),
            dma((4,)), dma((4,)),
            dma((54,)), dma((54,)),
            dma((9,)), dma((9,)),
            dma((21,)), dma((21,)),
            dma((21,)), dma((21,)),
            dma((2,)), dma((2,)),
            dma((7,)), dma((7,)),
        ],
        compiler_params=pltpu.CompilerParams(
            collective_id=0, has_side_effects=True, vmem_limit_bytes=60 << 20
        ),
        name="solve_steps",
    )(flags, right_sides, factor_panel, diag_inverse)


def solution(mesh):
    in_specs = (P("gr", "gc"), P(None, ("gr", "gc"), None), P(), P(), P())
    return jax.shard_map(shards, mesh=mesh, in_specs=in_specs, out_specs=P("gr", "gc"), check_vma=False)
```

```python
import jax
import jax.numpy as jnp
from jax import lax
from jax.experimental import pallas as pl
from jax.experimental.pallas import tpu as pltpu
from jax.sharding import PartitionSpec as P

MESH = pl.DeviceIdType.MESH
F32 = jnp.float32
BF16 = jnp.bfloat16
NB = 1024
HALF = 512
COLS = 128
ROW_PEERS = ((0, 1), (1, 0), (3, 0), (1, 1), (3, 1), (2, 0), (2, 1))
INVERSE = tuple(ROW_PEERS.index(((4 - dx) % 4, flip)) for dx, flip in ROW_PEERS)
ORDERS = ((0, 1, 2), (1, 2, 0), (2, 0, 1))


def dot(a, b):
    return jnp.dot(a, b, preferred_element_type=F32)


def kernel(
    steps_ref, ids_ref, rhs_ref, panel_ref, diag_ref, out_ref,
    flags, rhs, panel, diag, fin, w, fsl, r1, r2, r3,
    thl, a0, stage, a_in, a_half, a_z, a_piece, a_y, afull,
    yf, ysol, parts, g_full, acc, c_out, c_in,
    load_sem, out_sem, fin_s, fin_r, sel_s, sel_r, f_s, f_r, a_s, a_r,
    y_s, y_r, z_s, z_r, fw_s, fw_r, g_s, g_r, c_s, c_r,
):
    gr, gc = lax.axis_index("gr"), lax.axis_index("gc")
    z, y_hi, core = gr // 4, (gr // 2) % 2, gr % 2
    x, y_lo = gc // 2, gc % 2
    y = y_hi * 2 + y_lo
    other = 1 - core
    here = (x, y, z)

    def device(at, c):
        return (at[2] * 4 + (at[1] // 2) * 2 + c, at[0] * 2 + at[1] % 2)

    def along(axis, step):
        at = list(here)
        at[axis] = (at[axis] + step) % 4
        return device(at, core)

    def row_peer(i, sign):
        dx, flip = ROW_PEERS[i]
        return ((x + sign * dx + 4) % 4) * 2 + (y_lo + flip) % 2

    def send(src, dst, s, r, to):
        copy = pltpu.make_async_remote_copy(
            src_ref=src, dst_ref=dst, send_sem=s, recv_sem=r, device_id=to, device_id_type=MESH
        )
        copy.start()
        return copy

    def local(src, dst, sem):
        copy = pltpu.make_async_copy(src, dst, sem)
        copy.start()
        return copy

    partner = (gr + 1 - 2 * core, gc)
    mine = pl.ds(pl.multiple_of(core * HALF, HALF), HALF)
    theirs = pl.ds(pl.multiple_of(other * HALF, HALF), HALF)

    load_d = [local(diag_ref.at[0], diag.at[0], load_sem.at[0])]
    load_rhs = local(rhs_ref, rhs, load_sem.at[1])
    load_f = [local(panel_ref.at[t], panel.at[t], load_sem.at[2 + t]) for t in range(2)]
    load_d += [local(diag_ref.at[t], diag.at[t], load_sem.at[3 + t]) for t in (1, 2)]
    load_f.append(local(panel_ref.at[2], panel.at[2], load_sem.at[6]))

    group = [
        (((z + dz) % 4) * 4 + ((y_hi + dy) % 2) * 2 + (core + dk) % 2, gc)
        for dz in range(4) for dy in range(2) for dk in range(2)
    ][1:]
    peers = group + [(gr, row_peer(i, 1)) for i in range(7)]
    peers.append(device((x, (1 - y_hi) * 2 + 1 - y_lo, z), core))
    barrier = pltpu.get_barrier_semaphore()
    for peer in peers:
        pl.semaphore_signal(barrier, inc=1, device_id=peer, device_id_type=MESH)
    pl.semaphore_wait(barrier, len(peers))

    fin_copies = []
    for t in range(2):
        for h in range(2):
            i = t * 2 + h
            fin_copies.append(
                send(
                    panel_ref.at[t, theirs, pl.ds(h * HALF, HALF)],
                    fin.at[t, pl.ds(h * HALF, HALF)],
                    fin_s.at[i], fin_r.at[i], partner,
                )
            )

    lanes = lax.broadcasted_iota(jnp.int32, (1, 128), 1)
    ids = ids_ref[...]
    block = gr * 8 + gc
    beside = (gr + 1 - 2 * core) * 8 + gc
    my_id = jnp.sum(jnp.where(lanes == block, ids.astype(F32), 0.0), axis=1, keepdims=True)
    places = []
    for t in range(3):
        number = steps_ref[t]
        place = jnp.sum(jnp.where(ids == number, lanes.astype(F32), 0.0), axis=1, keepdims=True)
        places.append(jnp.broadcast_to(place, (1, 128)))
        pending = jnp.broadcast_to(my_id, (1, 128)).astype(jnp.int32) > number
        flags[28 + t:29 + t, :] = jnp.where(pending, 1.0, 0.0)
        for j in range(8):
            at = (gr * 8 + j).astype(F32)
            flags[t * 8 + j:t * 8 + j + 1, :] = jnp.where(places[t] == at, 1.0, 0.0)
    for row, t, at in ((24, 1, block), (25, 1, beside), (26, 2, block), (27, 2, beside)):
        flags[row:row + 1, :] = jnp.where(places[t] == at.astype(F32), 1.0, 0.0)

    def flag(row):
        return flags[row:row + 1, :]

    def build(slot, t, row):
        def mask(r):
            tile = jnp.broadcast_to(flag(r), (128, COLS)).astype(BF16)
            return jnp.concatenate([tile] * (HALF // COLS), axis=1)

        own, oth = mask(row), mask(row + 1)

        def chunk(i, carry):
            rows = pl.ds(pl.multiple_of(core * HALF + i * 128, 128), 128)
            for h in range(2):
                to = pl.ds(pl.multiple_of(h * HALF + i * 128, 128), 128)
                value = panel[t, rows, pl.ds(h * HALF, HALF)] * own + fin[t, to] * oth
                if slot == 0:
                    w[slot, to] = value
                else:
                    for m in range(8):
                        unit = pl.ds(pl.multiple_of(i * 256 + m * 32 + h * 16, 16), 16)
                        w[slot, unit] = value[m * 16:(m + 1) * 16]
            return carry

        lax.fori_loop(0, 4, chunk, 0)

    bases = []
    for slot in range(3):
        v = [here[a] for a in ORDERS[slot]]
        bases.append((v, (0, v[0] * 256, v[0] * 256 + v[1] * 64)))
    sizes = (256, 64, 16)

    def sem_at(slot, stage_no, step):
        return (slot * 3 + stage_no) * 3 + step - 1

    def scatter(slot, st):
        v, base = bases[slot]
        size = sizes[st]
        buf = (r1, r2, r3)[st]
        out = []
        for step in (1, 2, 3):
            rows = pl.ds(pl.multiple_of(base[st] + ((v[st] + step) % 4) * size, size), size)
            i = sem_at(slot, st, step)
            out.append(
                send(
                    w.at[slot, rows], buf.at[slot, step - 1], sel_s.at[i], sel_r.at[i],
                    along(ORDERS[slot][st], step),
                )
            )
        return out

    def total(slot, st, copies):
        v, base = bases[slot]
        size = sizes[st]
        buf = (r1, r2, r3)[st]
        for copy in copies:
            copy.wait()
        start = base[st] + v[st] * size
        span = min(size, 64)

        def chunk(i, carry):
            rows = pl.ds(pl.multiple_of(start + i * span, span), span)
            part = pl.ds(pl.multiple_of(i * span, span), span)
            value = w[slot, rows] + buf[slot, 0, part] + (buf[slot, 1, part] + buf[slot, 2, part])
            if st == 2:
                fsl[slot, gc] = value
            else:
                w[slot, rows] = value
            return carry

        lax.fori_loop(0, size // span, chunk, 0)

    def gather(slot):
        return [
            send(
                fsl.at[slot, gc], fsl.at[slot, gc], f_s.at[slot * 7 + i], f_r.at[slot * 7 + i],
                (gr, row_peer(i, 1)),
            )
            for i in range(7)
        ]

    def finish(copies):
        for copy in copies:
            copy.wait()

    def leading(t):
        def split(i, carry):
            rows = pl.ds(pl.multiple_of(i * 128, 128), 128)
            value = jnp.zeros((128, COLS), F32)
            for j in range(8):
                part = rhs[pl.ds(pl.multiple_of(j * NB + i * 128, 128), 128), :]
                value = jnp.where(flag(t * 8 + j) > 0.5, part, value)
            high = value.astype(BF16)
            thl[rows, pl.ds(0, COLS)] = high
            thl[rows, pl.ds(COLS, COLS)] = (value - high.astype(F32)).astype(BF16)
            return carry

        lax.fori_loop(0, 8, split, 0)

        def solve(i, carry):
            rows = pl.ds(pl.multiple_of(i * 256, 256), 256)
            both = dot(diag[t, rows], thl[...])
            value = both[:, :COLS] + both[:, COLS:]
            high = value.astype(BF16)
            if t == 0:
                a0[rows] = value
                stage[0, rows] = high
            else:
                stage[2 * t - 1, rows] = high
                stage[2 * t, rows] = (value - high.astype(F32)).astype(BF16)
            return carry

        lax.fori_loop(0, 4, solve, 0)

    spans = (pl.ds(0, 1), pl.ds(1, 4))
    members = (range(1), range(1, 5))
    z_rows = [pl.ds(pl.multiple_of(((z + step) % 4) * 128, 128), 128) for step in range(4)]
    piece = pl.ds(pl.multiple_of(core * HALF + z * 128, 128), 128)

    def a_sems(n, i):
        return a_s.at[n * 9 + i], a_r.at[n * 9 + i]

    def a_cores(n):
        return send(stage.at[spans[n], theirs], a_in.at[spans[n]], *a_sems(n, 0), partner)

    def a_join(n):
        for t in members[n]:
            a_half[t] = stage[t, mine] + a_in[t]

    def a_scatter(n):
        return [
            send(
                a_half.at[spans[n], z_rows[step]], a_z.at[step - 1, spans[n]],
                *a_sems(n, step), along(2, step),
            )
            for step in (1, 2, 3)
        ]

    def a_cross(n):
        for t in members[n]:
            a_piece[t] = a_half[t, z_rows[0]] + a_z[0, t] + (a_z[1, t] + a_z[2, t])
        return send(a_piece.at[spans[n]], a_y.at[spans[n]], *a_sems(n, 4), along(1, 2))

    def a_gather(n):
        for t in members[n]:
            afull[t, piece] = a_piece[t] + a_y[t]
        block_at = afull.at[spans[n], piece]
        return [
            send(block_at, block_at, *a_sems(n, 4 + step), along(2, step)) for step in (1, 2, 3)
        ]

    def a_share(n):
        block_at = afull.at[spans[n], mine]
        return send(block_at, block_at, *a_sems(n, 8), partner)

    def publish(t, rows):
        return [
            send(
                yf.at[t, gc, rows], yf.at[t, gc, rows], y_s.at[t * 7 + i], y_r.at[t * 7 + i],
                (gr, row_peer(i, 1)),
            )
            for i in range(7)
        ]

    def to_core(t, i):
        block_at = yf.at[t, row_peer(i, -1), mine]
        j = t * 7 + i
        return send(block_at, block_at, fw_s.at[j], fw_r.at[j], partner)

    run = [None] * 3
    load_d[0].wait()
    load_rhs.wait()
    leading(0)
    a_copy = a_cores(0)
    load_f[0].wait()
    finish(fin_copies[:2])
    build(0, 0, 24)
    run[0] = scatter(0, 0)
    build(1, 0, 26)
    run[1] = scatter(1, 0)
    a_copy.wait()
    a_join(0)
    z_copies = a_scatter(0)
    load_f[1].wait()
    finish(fin_copies[2:])
    build(2, 1, 26)
    run[2] = scatter(2, 0)
    for t in (1, 2):
        load_d[t].wait()
        leading(t)
    b_copy = a_cores(1)
    finish(z_copies)
    a_copy = a_cross(0)
    b_copy.wait()
    a_join(1)

    for slot in range(3):
        total(slot, 0, run[slot])
        run[slot] = scatter(slot, 1)
    a_copy.wait()
    z_copies = a_gather(0)
    b_copies = a_scatter(1)

    for slot in range(3):
        total(slot, 1, run[slot])
        run[slot] = scatter(slot, 2)
    finish(z_copies)
    a_copy = a_share(0)
    finish(b_copies)
    b_copy = a_cross(1)

    for slot in range(3):
        total(slot, 2, run[slot])
        run[slot] = gather(slot)
    a_copy.wait()
    yf[0, gc] = afull[0]
    y0_copies = publish(0, mine)
    b_copy.wait()
    b_copies = a_gather(1)

    def contribute(t):
        keep = jnp.concatenate([flag(28 + t)] * 2, axis=1) > 0.5

        def pair(i, carry):
            right = jnp.concatenate([yf[t, 2 * i], yf[t, 2 * i + 1]], axis=1)

            def tile(m, inner):
                rows = pl.ds(pl.multiple_of(m * 256, 256), 256)
                value = dot(panel[t, rows], right)
                value = jnp.where(keep, value, jnp.zeros_like(value))
                for e in range(2):
                    part = value[:, e * COLS:(e + 1) * COLS]
                    acc[2 * i + e, rows] = part
                return inner

            lax.fori_loop(0, 4, tile, 0)
            return carry

        lax.fori_loop(0, 4, pair, 0)

    lefts = ((0, 1, 2, 3), (0, 1, 4, 5), (0, 2, 4, 6))
    shift = (4, 2, 1)

    def product(n, t):
        low = jnp.concatenate([fsl[n, i] for i in lefts[n]], axis=0)
        high = jnp.concatenate([fsl[n, i + shift[n]] for i in lefts[n]], axis=0)
        value = dot(low, yf[t, gc, pl.ds(0, HALF)]) + dot(high, yf[t, gc, pl.ds(HALF, HALF)])
        parts[n, gr] = value.astype(BF16)
        return [
            send(parts.at[n, gr], parts.at[n, gr], g_s.at[n * 15 + i], g_r.at[n * 15 + i], group[i])
            for i in range(15)
        ]

    def unit_of(n, i, at_z, at_y):
        if n == 0:
            return (i >> 1) * 16 + at_y * 8 + (i & 1) * 4 + at_z
        if n == 1:
            return (at_y * 2 + (i & 1)) * 8 + at_z * 2 + (i >> 1)
        return at_z * 8 + i * 2 + at_y

    def assemble(n):
        for source in range(16):
            for i in range(4):
                unit = (source % 2) * 32 + unit_of(n, i, source // 4, (source // 2) % 2)
                g_full[pl.ds(unit * 16, 16), pl.ds((n // 2) * COLS, COLS)] = parts[
                    n, source, pl.ds(i * 16, 16)
                ]

    def next_y(t):
        def tile(i, carry):
            rows = pl.ds(pl.multiple_of(i * 256, 256), 256)
            value = afull[2 * t - 1, rows].astype(F32) + afull[2 * t, rows].astype(F32)
            change = dot(diag[t, rows], g_full[:, pl.ds(0, t * COLS)])
            for e in range(t):
                value = value - change[:, e * COLS:(e + 1) * COLS]
            ysol[t - 1, rows] = value
            yf[t, gc, rows] = value.astype(BF16)
            return carry

        lax.fori_loop(0, 4, tile, 0)

    finish(run[0])
    g_copies = [product(0, 0)]
    finish(run[1])
    g_copies.append(product(1, 0))
    finish(b_copies)
    b_copy = a_share(1)
    finish(g_copies[0])
    assemble(0)
    b_copy.wait()
    next_y(1)
    quarter = piece
    y1_copies = publish(1, quarter)
    finish(run[2])
    g_copies.append(product(2, 1))
    z_copies = []
    for i in range(7):
        y1_copies[i].wait()
        block_at = yf.at[1, row_peer(i, -1), quarter]
        z_copies.append(
            [
                send(block_at, block_at, z_s.at[i * 3 + step - 1], z_r.at[i * 3 + step - 1], along(2, step))
                for step in (1, 2, 3)
            ]
        )
    finish(g_copies[1])
    assemble(1)
    finish(g_copies[2])
    assemble(2)
    next_y(2)
    y2_copies = publish(2, mine)

    forwards = []
    for i in range(7):
        y0_copies[i].wait()
        forwards.append(to_core(0, i))
    finish(forwards)
    contribute(0)
    forwards1 = []
    for i in range(7):
        finish(z_copies[i])
        forwards1.append(to_core(1, i))

    load_f[2].wait()
    keep1, keep2 = flag(29) > 0.5, flag(30) > 0.5

    def last(col, put):
        def tile(m, inner):
            rows = pl.ds(pl.multiple_of(m * 256, 256), 256)
            value = acc[col, rows]
            for t, keep in ((1, keep1), (2, keep2)):
                change = dot(panel[t, rows], yf[t, col])
                value = value + jnp.where(keep, change, jnp.zeros_like(change))
            put(rows, value.astype(BF16))
            return inner

        lax.fori_loop(0, 4, tile, 0)

    def put_own(rows, value):
        c_in[gc, rows] = value

    last(gc, put_own)
    c_copies = [None] * 7
    y2_copies[0].wait()
    ahead = to_core(2, 0)
    for i in range(7):
        arrived = ahead
        if i < 6:
            y2_copies[i + 1].wait()
            ahead = to_core(2, i + 1)
        forwards1[i].wait()
        arrived.wait()
        to = INVERSE[i]
        col = row_peer(i, -1)

        def put(rows, value, to=to):
            c_out[to, rows] = value

        last(col, put)
        c_copies[to] = send(c_out.at[to], c_in.at[gc], c_s.at[to], c_r.at[to], (gr, col))

    def settle(j):
        def tile(m, inner):
            rows = pl.ds(pl.multiple_of(j * NB + m * 256, 256), 256)
            part = pl.ds(pl.multiple_of(m * 256, 256), 256)
            value = rhs[rows, :] - c_in[j, part].astype(F32)
            for t, solved in enumerate((a0[part], ysol[0, part], ysol[1, part])):
                value = jnp.where(flags[pl.ds(t * 8 + j, 1), :] > 0.5, solved, value)
            rhs[rows, :] = value
            return inner

        lax.fori_loop(0, 4, tile, 0)
        rows = pl.ds(pl.multiple_of(j * NB, NB), NB)
        return rows

    stores = []
    rows = settle(gc)
    stores.append(local(rhs.at[rows], out_ref.at[rows], out_sem.at[7]))
    for i in range(7):
        c_copies[i].wait()
        rows = settle(row_peer(i, -1))
        stores.append(local(rhs.at[rows], out_ref.at[rows], out_sem.at[i]))
    finish(stores)


def shards(right_sides, factor_panel, diag_inverse, block_ids, step_blocks):
    dma = pltpu.SemaphoreType.DMA
    vm = pltpu.VMEM
    return pl.pallas_call(
        kernel,
        out_shape=jax.ShapeDtypeStruct((8 * NB, COLS), F32),
        in_specs=[pl.BlockSpec(memory_space=pltpu.SMEM), pl.BlockSpec(memory_space=pltpu.VMEM)]
        + [pl.BlockSpec(memory_space=pl.ANY)] * 3,
        out_specs=pl.BlockSpec(memory_space=pl.ANY),
        scratch_shapes=[
            vm((32, COLS), F32),
            vm((8 * NB, COLS), F32),
            vm((3, NB, NB), BF16),
            vm((3, NB, NB), BF16),
            vm((2, NB, HALF), BF16),
            vm((3, NB, HALF), BF16),
            vm((3, 8, 16, HALF), BF16),
            vm((3, 3, 256, HALF), BF16),
            vm((3, 3, 64, HALF), BF16),
            vm((3, 3, 16, HALF), BF16),
            vm((NB, 2 * COLS), BF16),
            vm((NB, COLS), F32),
            vm((5, NB, COLS), BF16),
            vm((5, HALF, COLS), BF16),
            vm((5, HALF, COLS), BF16),
            vm((3, 5, 128, COLS), BF16),
            vm((5, 128, COLS), BF16),
            vm((5, 128, COLS), BF16),
            vm((5, NB, COLS), BF16),
            vm((3, 8, NB, COLS), BF16),
            vm((2, NB, COLS), F32),
            vm((3, 16, 64, COLS), BF16),
            vm((NB, 2 * COLS), BF16),
            vm((8, NB, COLS), F32),
            vm((7, NB, COLS), BF16),
            vm((8, NB, COLS), BF16),
            dma((7,)), dma((8,)),
            dma((4,)), dma((4,)),
            dma((27,)), dma((27,)),
            dma((21,)), dma((21,)),
            dma((18,)), dma((18,)),
            dma((21,)), dma((21,)),
            dma((21,)), dma((21,)),
            dma((21,)), dma((21,)),
            dma((45,)), dma((45,)),
            dma((7,)), dma((7,)),
        ],
        compiler_params=pltpu.CompilerParams(
            collective_id=0, has_side_effects=True, vmem_limit_bytes=60 << 20
        ),
        name="solve_steps",
    )(step_blocks, block_ids.reshape(1, 128), right_sides, factor_panel, diag_inverse)


def solution(mesh):
    in_specs = (P("gr", "gc"), P(None, ("gr", "gc"), None), P(), P(), P())
    return jax.shard_map(shards, mesh=mesh, in_specs=in_specs, out_specs=P("gr", "gc"), check_vma=False)
```

```python
import jax
import jax.numpy as jnp
from jax import lax
from jax.experimental import pallas as pl
from jax.experimental.pallas import tpu as pltpu
from jax.sharding import PartitionSpec as P

MESH = pl.DeviceIdType.MESH
F32 = jnp.float32
BF16 = jnp.bfloat16
NB = 1024
HALF = 512
COLS = 128
ROW_PEERS = ((2, 0), (1, 0), (3, 0), (0, 1), (2, 1), (1, 1), (3, 1))
ALONG_X = range(3)
DIRECT = range(4)
ACROSS = range(4, 7)
LAST = (3, 0, 4, 1, 5, 2, 6)
INVERSE = tuple(ROW_PEERS.index(((4 - dx) % 4, flip)) for dx, flip in ROW_PEERS)
ORDERS = ((0, 1, 2), (1, 2, 0), (2, 0, 1))


def dot(a, b):
    return jnp.dot(a, b, preferred_element_type=F32)


def kernel(
    steps_ref, ids_ref, rhs_ref, panel_ref, diag_ref, out_ref,
    flags, rhs, panel, diag, fin, w, fsl, r1, r2, r3,
    thl, a0, stage, a_in, a_half, a_z, a_piece, a_y, tst, t_in, t_half, t_z, t_piece, t_y,
    yf, ysol, g_full, c_out, c_in,
    load_sem, out_sem, fin_s, fin_r, sel_s, sel_r, f_s, f_r, a_s, a_r, t_s, t_r,
    y_s, y_r, z_s, z_r, fw_s, fw_r, g_s, g_r, h_s, h_r, c_s, c_r,
):
    gr, gc = lax.axis_index("gr"), lax.axis_index("gc")
    z, y_hi, core = gr // 4, (gr // 2) % 2, gr % 2
    x, y_lo = gc // 2, gc % 2
    y = y_hi * 2 + y_lo
    other = 1 - core
    here = (x, y, z)

    def device(at, c):
        return (at[2] * 4 + (at[1] // 2) * 2 + c, at[0] * 2 + at[1] % 2)

    def along(axis, step):
        at = list(here)
        at[axis] = (at[axis] + step) % 4
        return device(at, core)

    def row_peer(i, sign):
        dx, flip = ROW_PEERS[i]
        return ((x + sign * dx + 4) % 4) * 2 + (y_lo + flip) % 2

    def send(src, dst, s, r, to):
        copy = pltpu.make_async_remote_copy(
            src_ref=src, dst_ref=dst, send_sem=s, recv_sem=r, device_id=to, device_id_type=MESH
        )
        copy.start()
        return copy

    def local(src, dst, sem):
        copy = pltpu.make_async_copy(src, dst, sem)
        copy.start()
        return copy

    partner = (gr + 1 - 2 * core, gc)
    mine = pl.ds(pl.multiple_of(core * HALF, HALF), HALF)
    theirs = pl.ds(pl.multiple_of(other * HALF, HALF), HALF)

    load_d = [local(diag_ref.at[0], diag.at[0], load_sem.at[0])]
    load_rhs = local(rhs_ref, rhs, load_sem.at[1])
    load_f = [local(panel_ref.at[t], panel.at[t], load_sem.at[2 + t]) for t in range(2)]
    load_d += [local(diag_ref.at[t], diag.at[t], load_sem.at[3 + t]) for t in (1, 2)]
    load_f.append(local(panel_ref.at[2], panel.at[2], load_sem.at[6]))

    steps = [(dz, dy) for dz in range(4) for dy in range(2)][1:]
    group = [(((z + dz) % 4) * 4 + ((y_hi + dy) % 2) * 2 + core, gc) for dz, dy in steps]
    peers = group + [(gr, row_peer(i, 1)) for i in range(7)]
    peers += [device((x, (1 - y_hi) * 2 + 1 - y_lo, z), core), partner]
    barrier = pltpu.get_barrier_semaphore()
    for peer in peers:
        pl.semaphore_signal(barrier, inc=1, device_id=peer, device_id_type=MESH)
    pl.semaphore_wait(barrier, len(peers))

    fin_copies = []
    for t in range(2):
        for h in range(2):
            i = t * 2 + h
            fin_copies.append(
                send(
                    panel_ref.at[t, theirs, pl.ds(h * HALF, HALF)],
                    fin.at[t, pl.ds(h * HALF, HALF)],
                    fin_s.at[i], fin_r.at[i], partner,
                )
            )

    lanes = lax.broadcasted_iota(jnp.int32, (1, 128), 1)
    ids = ids_ref[...]
    block = gr * 8 + gc
    beside = (gr + 1 - 2 * core) * 8 + gc
    my_id = jnp.sum(jnp.where(lanes == block, ids.astype(F32), 0.0), axis=1, keepdims=True)
    places = []
    for t in range(3):
        number = steps_ref[t]
        place = jnp.sum(jnp.where(ids == number, lanes.astype(F32), 0.0), axis=1, keepdims=True)
        places.append(jnp.broadcast_to(place, (1, 128)))
        pending = jnp.broadcast_to(my_id, (1, 128)).astype(jnp.int32) > number
        flags[28 + t:29 + t, :] = jnp.where(pending, 1.0, 0.0)
        for j in range(8):
            at = (gr * 8 + j).astype(F32)
            flags[t * 8 + j:t * 8 + j + 1, :] = jnp.where(places[t] == at, 1.0, 0.0)
    for row, t, at in ((24, 1, block), (25, 1, beside), (26, 2, block), (27, 2, beside)):
        flags[row:row + 1, :] = jnp.where(places[t] == at.astype(F32), 1.0, 0.0)

    def flag(row):
        return flags[row:row + 1, :]

    def build(slot, t, row):
        def mask(r):
            tile = jnp.broadcast_to(flag(r), (128, COLS)).astype(BF16)
            return jnp.concatenate([tile] * (HALF // COLS), axis=1)

        own, oth = mask(row), mask(row + 1)

        def chunk(i, carry):
            rows = pl.ds(pl.multiple_of(core * HALF + i * 128, 128), 128)
            for h in range(2):
                to = pl.ds(pl.multiple_of(h * HALF + i * 128, 128), 128)
                value = panel[t, rows, pl.ds(h * HALF, HALF)] * own + fin[t, to] * oth
                for m in range(8):
                    at = (m % 2 * 2 + h, i, m // 2)
                    first, second, third = (at[a] for a in ORDERS[slot])
                    unit = pl.ds(pl.multiple_of((first * 16 + second * 4 + third) * 16, 16), 16)
                    w[slot, unit] = value[m * 16:(m + 1) * 16]
            return carry

        lax.fori_loop(0, 4, chunk, 0)

    bases = []
    for slot in range(3):
        v = [here[a] for a in ORDERS[slot]]
        bases.append((v, (0, v[0] * 256, v[0] * 256 + v[1] * 64)))
    sizes = (256, 64, 16)

    def sem_at(slot, stage_no, step):
        return (slot * 3 + stage_no) * 3 + step - 1

    def scatter(slot, st):
        v, base = bases[slot]
        size = sizes[st]
        buf = (r1, r2, r3)[st]
        out = []
        for step in (1, 2, 3):
            rows = pl.ds(pl.multiple_of(base[st] + ((v[st] + step) % 4) * size, size), size)
            i = sem_at(slot, st, step)
            out.append(
                send(
                    w.at[slot, rows], buf.at[slot, step - 1], sel_s.at[i], sel_r.at[i],
                    along(ORDERS[slot][st], step),
                )
            )
        return out

    def total(slot, st, copies):
        v, base = bases[slot]
        size = sizes[st]
        buf = (r1, r2, r3)[st]
        for copy in copies:
            copy.wait()
        start = base[st] + v[st] * size
        span = min(size, 64)

        def chunk(i, carry):
            rows = pl.ds(pl.multiple_of(start + i * span, span), span)
            part = pl.ds(pl.multiple_of(i * span, span), span)
            value = w[slot, rows] + buf[slot, 0, part] + (buf[slot, 1, part] + buf[slot, 2, part])
            if st == 2:
                fsl[slot, gc] = value
            else:
                w[slot, rows] = value
            return carry

        lax.fori_loop(0, size // span, chunk, 0)

    def gather(slot):
        return [
            send(
                fsl.at[slot, gc], fsl.at[slot, gc], f_s.at[slot * 7 + i], f_r.at[slot * 7 + i],
                (gr, row_peer(i, 1)),
            )
            for i in range(7)
        ]

    def finish(copies):
        for copy in copies:
            copy.wait()

    def target(t, i):
        value = jnp.zeros((128, COLS), F32)
        for j in range(8):
            part = rhs[pl.ds(pl.multiple_of(j * NB + i * 128, 128), 128), :]
            value = jnp.where(flag(t * 8 + j) > 0.5, part, value)
        high = value.astype(BF16)
        return high, (value - high.astype(F32)).astype(BF16)

    def leading():
        def split(i, carry):
            rows = pl.ds(pl.multiple_of(i * 128, 128), 128)
            thl[rows, pl.ds(0, COLS)], thl[rows, pl.ds(COLS, COLS)] = target(0, i)
            return carry

        lax.fori_loop(0, 8, split, 0)

        def solve(i, carry):
            rows = pl.ds(pl.multiple_of(i * 256, 256), 256)
            both = dot(diag[0, rows], thl[...])
            value = both[:, :COLS] + both[:, COLS:]
            a0[rows] = value
            stage[rows] = value.astype(BF16)
            return carry

        lax.fori_loop(0, 4, solve, 0)

    def later_targets():
        for t in (1, 2):
            def split(i, carry, t=t):
                for e, term in enumerate(target(t, i)):
                    for q in range(4):
                        tst[t * 2 - 2 + e, i, q] = term[q * 32:(q + 1) * 32]
                return carry

            lax.fori_loop(0, 8, split, 0)

    z_rows = [pl.ds(pl.multiple_of(((z + step) % 4) * 128, 128), 128) for step in range(4)]
    piece = pl.ds(pl.multiple_of(core * HALF + z * 128, 128), 128)

    def a_cores():
        return send(stage.at[theirs], a_in, a_s.at[0], a_r.at[0], partner)

    def a_scatter():
        a_half[...] = stage[mine] + a_in[...]
        return [
            send(a_half.at[z_rows[step]], a_z.at[step - 1], a_s.at[step], a_r.at[step], along(2, step))
            for step in (1, 2, 3)
        ]

    def a_cross():
        a_piece[...] = a_half[z_rows[0]] + a_z[0] + (a_z[1] + a_z[2])
        return send(a_piece, a_y, a_s.at[4], a_r.at[4], along(1, 2))

    def a_gather():
        yf[0, gc, piece] = a_piece[...] + a_y[...]
        block_at = yf.at[0, gc, piece]
        return [
            send(block_at, block_at, a_s.at[4 + step], a_r.at[4 + step], along(2, step))
            for step in (1, 2, 3)
        ]

    def a_share():
        block_at = yf.at[0, gc, mine]
        return send(block_at, block_at, a_s.at[8], a_r.at[8], partner)

    my_four = pl.ds(core * 4, 4)

    def t_cores():
        return send(tst.at[:, pl.ds(other * 4, 4)], t_in, t_s.at[0], t_r.at[0], partner)

    def t_scatter():
        for e in range(4):
            t_half[e] = tst[e, my_four] + t_in[e]
        return [
            send(
                t_half.at[:, :, (z + step) % 4], t_z.at[step - 1], t_s.at[step], t_r.at[step],
                along(2, step),
            )
            for step in (1, 2, 3)
        ]

    def t_cross():
        for e in range(4):
            t_piece[e] = t_half[e, :, z] + t_z[0, e] + (t_z[1, e] + t_z[2, e])
        return send(t_piece.at[:, pl.ds((1 - y_hi) * 2, 2)], t_y, t_s.at[4], t_r.at[4], along(1, 2))

    def t_own(t):
        value = jnp.zeros((2, 32, COLS), F32)
        for e in (2 * t - 2, 2 * t - 1):
            value = value + (t_piece[e, pl.ds(y_hi * 2, 2)] + t_y[e]).astype(F32)
        return value.reshape(64, COLS)

    def publish(t, which):
        copies = {}
        for i in which:
            rows = mine if i in DIRECT else piece
            block_at = yf.at[t, gc, rows]
            j = t * 7 + i
            copies[i] = send(block_at, block_at, y_s.at[j], y_r.at[j], (gr, row_peer(i, 1)))
        return copies

    def relay(t, copies):
        out = {}
        for i in ACROSS:
            copies[i].wait()
            block_at = yf.at[t, row_peer(i, -1), piece]
            j = (t * 3 + i - 4) * 3 - 1
            out[i] = [
                send(block_at, block_at, z_s.at[j + step], z_r.at[j + step], along(2, step))
                for step in (1, 2, 3)
            ]
        return out

    def arrive(copies, relays, i):
        if i in DIRECT:
            copies[i].wait()
        else:
            finish(relays[i])

    def to_core(t, i):
        block_at = yf.at[t, row_peer(i, -1), mine]
        j = t * 7 + i
        return send(block_at, block_at, fw_s.at[j], fw_r.at[j], partner)

    run = [None] * 3
    load_d[0].wait()
    load_rhs.wait()
    leading()
    a_copy = a_cores()
    load_f[0].wait()
    finish(fin_copies[:2])
    build(0, 0, 24)
    run[0] = scatter(0, 0)
    build(1, 0, 26)
    run[1] = scatter(1, 0)
    a_copy.wait()
    z_copies = a_scatter()
    load_f[1].wait()
    finish(fin_copies[2:])
    build(2, 1, 26)
    run[2] = scatter(2, 0)
    later_targets()
    t_copy = t_cores()
    finish(z_copies)
    a_copy = a_cross()

    for slot in range(3):
        total(slot, 0, run[slot])
        run[slot] = scatter(slot, 1)
    a_copy.wait()
    z_copies = a_gather()
    t_copy.wait()
    t_copies = t_scatter()

    for slot in range(3):
        total(slot, 1, run[slot])
        run[slot] = scatter(slot, 2)
    finish(z_copies)
    a_copy = a_share()
    finish(t_copies)
    t_copy = t_cross()

    for slot in range(3):
        total(slot, 2, run[slot])
        run[slot] = gather(slot)
    a_copy.wait()
    t_copy.wait()

    def product(slot, t):
        low = jnp.concatenate([fsl[slot, (i % 2) * 4 + i // 2] for i in range(4)], axis=0)
        high = jnp.concatenate([fsl[slot, (i % 2) * 4 + i // 2 + 2] for i in range(4)], axis=0)
        value = dot(low, yf[t, gc, pl.ds(0, HALF)]) + dot(high, yf[t, gc, pl.ds(HALF, HALF)])
        return value.astype(BF16).astype(F32)

    def spread(n, value):
        high = value.astype(BF16)
        both = jnp.concatenate([high, (value - high.astype(F32)).astype(BF16)], axis=1)
        for e in range(2):
            g_full[n, core, y_hi, e, z] = both[e * 32:(e + 1) * 32]
        block_at = g_full.at[n, core, y_hi, :, z]
        copies = [
            send(block_at, block_at, g_s.at[n * 7 + i], g_r.at[n * 7 + i], group[i]) for i in range(7)
        ]
        copies.append(send(block_at, block_at, h_s.at[n * 8 + 7], h_r.at[n * 8 + 7], partner))
        return copies

    def collect_spread(n, copies):
        shared = [copies[7]]
        for i, (dz, dy) in enumerate(steps):
            copies[i].wait()
            block_at = g_full.at[n, core, (y_hi + dy) % 2, :, (z + 4 - dz) % 4]
            shared.append(send(block_at, block_at, h_s.at[n * 8 + i], h_r.at[n * 8 + i], partner))
        finish(shared)

    def next_y(t):
        right = g_full[t - 1].reshape(NB, 2 * COLS)

        def tile(i, carry):
            rows = pl.ds(pl.multiple_of(i * 256, 256), 256)
            both = dot(diag[t, rows], right)
            value = both[:, :COLS] + both[:, COLS:]
            ysol[t - 1, rows] = value
            yf[t, gc, rows] = value.astype(BF16)
            return carry

        lax.fori_loop(0, 4, tile, 0)

    finish(run[0])
    s_copies = spread(0, t_own(1) - product(0, 0))
    y_copies = [publish(0, range(7)), None, None]
    relays = [None] * 3
    finish(run[1])
    second = t_own(2) - product(1, 0)
    load_d[1].wait()
    load_d[2].wait()
    collect_spread(0, s_copies)
    next_y(1)
    finish(run[2])
    s_copies = spread(1, second - product(2, 1))
    y_copies[1] = publish(1, range(7))
    relays[0] = relay(0, y_copies[0])
    collect_spread(1, s_copies)
    next_y(2)
    y_copies[2] = publish(2, (3, 4, 5, 6, 0, 1, 2))
    relays[1] = relay(1, y_copies[1])

    load_f[2].wait()
    keeps = [flag(28 + t) > 0.5 for t in range(3)]

    def last(col, put):
        def tile(m, inner):
            rows = pl.ds(pl.multiple_of(m * 256, 256), 256)
            value = jnp.zeros((256, COLS), F32)
            for t in range(3):
                change = dot(panel[t, rows], yf[t, col])
                value = value + jnp.where(keeps[t], change, jnp.zeros_like(change))
            put(rows, value.astype(BF16))
            return inner

        lax.fori_loop(0, 4, tile, 0)

    def put_own(rows, value):
        c_in[gc, rows] = value

    last(gc, put_own)
    c_copies = [None] * 7

    def collect(i):
        out = []
        for t in range(3):
            arrive(y_copies[t], relays[t], i)
            out.append(to_core(t, i))
        return out

    ahead = collect(LAST[0])
    relays[2] = relay(2, y_copies[2])
    for n, i in enumerate(LAST):
        arrived = ahead
        if n < 6:
            ahead = collect(LAST[n + 1])
        finish(arrived)
        to = INVERSE[i]
        col = row_peer(i, -1)

        def put(rows, value, to=to):
            c_out[to, rows] = value

        last(col, put)
        c_copies[to] = send(c_out.at[to], c_in.at[gc], c_s.at[to], c_r.at[to], (gr, col))

    def settle(j):
        def tile(m, inner):
            rows = pl.ds(pl.multiple_of(j * NB + m * 256, 256), 256)
            part = pl.ds(pl.multiple_of(m * 256, 256), 256)
            value = rhs[rows, :] - c_in[j, part].astype(F32)
            for t, solved in enumerate((a0[part], ysol[0, part], ysol[1, part])):
                value = jnp.where(flags[pl.ds(t * 8 + j, 1), :] > 0.5, solved, value)
            rhs[rows, :] = value
            return inner

        lax.fori_loop(0, 4, tile, 0)
        rows = pl.ds(pl.multiple_of(j * NB, NB), NB)
        return rows

    stores = []
    rows = settle(gc)
    stores.append(local(rhs.at[rows], out_ref.at[rows], out_sem.at[7]))
    for i in (INVERSE[n] for n in LAST):
        c_copies[i].wait()
        rows = settle(row_peer(i, -1))
        stores.append(local(rhs.at[rows], out_ref.at[rows], out_sem.at[i]))
    finish(stores)


def shards(right_sides, factor_panel, diag_inverse, block_ids, step_blocks):
    dma = pltpu.SemaphoreType.DMA
    vm = pltpu.VMEM
    return pl.pallas_call(
        kernel,
        out_shape=jax.ShapeDtypeStruct((8 * NB, COLS), F32),
        in_specs=[pl.BlockSpec(memory_space=pltpu.SMEM), pl.BlockSpec(memory_space=pltpu.VMEM)]
        + [pl.BlockSpec(memory_space=pl.ANY)] * 3,
        out_specs=pl.BlockSpec(memory_space=pl.ANY),
        scratch_shapes=[
            vm((32, COLS), F32),
            vm((8 * NB, COLS), F32),
            vm((3, NB, NB), BF16),
            vm((3, NB, NB), BF16),
            vm((2, NB, HALF), BF16),
            vm((3, NB, HALF), BF16),
            vm((3, 8, 16, HALF), BF16),
            vm((3, 3, 256, HALF), BF16),
            vm((3, 3, 64, HALF), BF16),
            vm((3, 3, 16, HALF), BF16),
            vm((NB, 2 * COLS), BF16),
            vm((NB, COLS), F32),
            vm((NB, COLS), BF16),
            vm((HALF, COLS), BF16),
            vm((HALF, COLS), BF16),
            vm((3, 128, COLS), BF16),
            vm((128, COLS), BF16),
            vm((128, COLS), BF16),
            vm((4, 8, 4, 32, COLS), BF16),
            vm((4, 4, 4, 32, COLS), BF16),
            vm((4, 4, 4, 32, COLS), BF16),
            vm((3, 4, 4, 32, COLS), BF16),
            vm((4, 4, 32, COLS), BF16),
            vm((4, 2, 32, COLS), BF16),
            vm((3, 8, NB, COLS), BF16),
            vm((2, NB, COLS), F32),
            vm((2, 2, 2, 2, 4, 32, 2 * COLS), BF16),
            vm((7, NB, COLS), BF16),
            vm((8, NB, COLS), BF16),
            dma((7,)), dma((8,)),
            dma((4,)), dma((4,)),
            dma((27,)), dma((27,)),
            dma((21,)), dma((21,)),
            dma((9,)), dma((9,)),
            dma((5,)), dma((5,)),
            dma((21,)), dma((21,)),
            dma((27,)), dma((27,)),
            dma((21,)), dma((21,)),
            dma((14,)), dma((14,)),
            dma((16,)), dma((16,)),
            dma((7,)), dma((7,)),
        ],
        compiler_params=pltpu.CompilerParams(
            collective_id=0, has_side_effects=True, vmem_limit_bytes=60 << 20
        ),
        name="solve_steps",
    )(step_blocks, block_ids.reshape(1, 128), right_sides, factor_panel, diag_inverse)


def solution(mesh):
    in_specs = (P("gr", "gc"), P(None, ("gr", "gc"), None), P(), P(), P())
    return jax.shard_map(shards, mesh=mesh, in_specs=in_specs, out_specs=P("gr", "gc"), check_vma=False)
```

```python
import jax
import jax.numpy as jnp
from jax import lax
from jax.experimental import pallas as pl
from jax.experimental.pallas import tpu as pltpu
from jax.sharding import PartitionSpec as P

MESH = pl.DeviceIdType.MESH
F32 = jnp.float32
BF16 = jnp.bfloat16
NB = 1024
HALF = 512
COLS = 128
ROW_PEERS = ((2, 0), (1, 0), (3, 0), (0, 1), (2, 1), (1, 1), (3, 1))
ALONG_X = range(3)
DIRECT = range(4)
ACROSS = range(4, 7)
LAST = (3, 0, 4, 1, 5, 2, 6)
INVERSE = tuple(ROW_PEERS.index(((4 - dx) % 4, flip)) for dx, flip in ROW_PEERS)
ORDERS = ((0, 1, 2), (1, 2, 0), (2, 0, 1)) * 2
BLOCK = (0, 0, 1, 1, 2, 2)
FIRST, SECOND = range(3), range(3, 6)
WIDE = 256


def dot(a, b):
    return jnp.dot(a, b, preferred_element_type=F32)


def kernel(
    steps_ref, ids_ref, rhs_ref, panel_ref, diag_ref, out_ref,
    flags, rhs, panel, diag, fin, w, fsl, r1, r2, r3,
    thl, a0, stage, a_in, a_half, a_z, a_piece, a_y, tst, t_in, t_half, t_z, t_piece, t_y,
    yf, ysol, g_full, c_out, c_in,
    load_sem, out_sem, fin_s, fin_r, sel_s, sel_r, f_s, f_r, a_s, a_r, t_s, t_r,
    y_s, y_r, z_s, z_r, fw_s, fw_r, g_s, g_r, h_s, h_r, c_s, c_r,
):
    gr, gc = lax.axis_index("gr"), lax.axis_index("gc")
    z, y_hi, core = gr // 4, (gr // 2) % 2, gr % 2
    x, y_lo = gc // 2, gc % 2
    y = y_hi * 2 + y_lo
    other = 1 - core
    here = (x, y, z)

    def device(at, c):
        return (at[2] * 4 + (at[1] // 2) * 2 + c, at[0] * 2 + at[1] % 2)

    def along(axis, step):
        at = list(here)
        at[axis] = (at[axis] + step) % 4
        return device(at, core)

    def row_peer(i, sign):
        dx, flip = ROW_PEERS[i]
        return ((x + sign * dx + 4) % 4) * 2 + (y_lo + flip) % 2

    def send(src, dst, s, r, to):
        copy = pltpu.make_async_remote_copy(
            src_ref=src, dst_ref=dst, send_sem=s, recv_sem=r, device_id=to, device_id_type=MESH
        )
        copy.start()
        return copy

    def local(src, dst, sem):
        copy = pltpu.make_async_copy(src, dst, sem)
        copy.start()
        return copy

    partner = (gr + 1 - 2 * core, gc)
    mine = pl.ds(pl.multiple_of(core * HALF, HALF), HALF)
    theirs = pl.ds(pl.multiple_of(other * HALF, HALF), HALF)

    load_d = [local(diag_ref.at[0], diag.at[0], load_sem.at[0])]
    load_rhs = local(rhs_ref, rhs, load_sem.at[1])
    load_f = [local(panel_ref.at[t], panel.at[t], load_sem.at[2 + t]) for t in range(2)]
    load_d += [local(diag_ref.at[t], diag.at[t], load_sem.at[3 + t]) for t in (1, 2)]
    load_f.append(local(panel_ref.at[2], panel.at[2], load_sem.at[6]))

    steps = [(dz, dy) for dz in range(4) for dy in range(2)][1:]
    group = [(((z + dz) % 4) * 4 + ((y_hi + dy) % 2) * 2 + core, gc) for dz, dy in steps]
    peers = group + [(gr, row_peer(i, 1)) for i in range(7)]
    peers += [device((x, (1 - y_hi) * 2 + 1 - y_lo, z), core), partner]
    barrier = pltpu.get_barrier_semaphore()
    for peer in peers:
        pl.semaphore_signal(barrier, inc=1, device_id=peer, device_id_type=MESH)
    pl.semaphore_wait(barrier, len(peers))

    fin_copies = []
    for t in range(2):
        for h in range(2):
            i = t * 2 + h
            fin_copies.append(
                send(
                    panel_ref.at[t, theirs, pl.ds(h * HALF, HALF)],
                    fin.at[t, pl.ds(h * HALF, HALF)],
                    fin_s.at[i], fin_r.at[i], partner,
                )
            )

    lanes = lax.broadcasted_iota(jnp.int32, (1, 128), 1)
    ids = ids_ref[...]
    block = gr * 8 + gc
    beside = (gr + 1 - 2 * core) * 8 + gc
    my_id = jnp.sum(jnp.where(lanes == block, ids.astype(F32), 0.0), axis=1, keepdims=True)
    places = []
    for t in range(3):
        number = steps_ref[t]
        place = jnp.sum(jnp.where(ids == number, lanes.astype(F32), 0.0), axis=1, keepdims=True)
        places.append(jnp.broadcast_to(place, (1, 128)))
        pending = jnp.broadcast_to(my_id, (1, 128)).astype(jnp.int32) > number
        flags[28 + t:29 + t, :] = jnp.where(pending, 1.0, 0.0)
        for j in range(8):
            at = (gr * 8 + j).astype(F32)
            flags[t * 8 + j:t * 8 + j + 1, :] = jnp.where(places[t] == at, 1.0, 0.0)
    for row, t, at in ((24, 1, block), (25, 1, beside), (26, 2, block), (27, 2, beside)):
        flags[row:row + 1, :] = jnp.where(places[t] == at.astype(F32), 1.0, 0.0)

    def flag(row):
        return flags[row:row + 1, :]

    def build(part, t, row):
        col = part % 2 * WIDE

        def mask(r):
            tile = jnp.broadcast_to(flag(r), (128, COLS)).astype(BF16)
            return jnp.concatenate([tile] * (WIDE // COLS), axis=1)

        own, oth = mask(row), mask(row + 1)

        def chunk(i, carry):
            rows = pl.ds(pl.multiple_of(core * HALF + i * 128, 128), 128)
            for h in range(2):
                to = pl.ds(pl.multiple_of(h * HALF + i * 128, 128), 128)
                value = (
                    panel[t, rows, pl.ds(h * HALF + col, WIDE)] * own
                    + fin[t, to, pl.ds(col, WIDE)] * oth
                )
                for m in range(8):
                    at = (m % 2 * 2 + h, i, m // 2)
                    first, second, third = (at[a] for a in ORDERS[part])
                    unit = pl.ds(pl.multiple_of((first * 16 + second * 4 + third) * 16, 16), 16)
                    w[part, unit] = value[m * 16:(m + 1) * 16]
            return carry

        lax.fori_loop(0, 4, chunk, 0)

    bases = []
    for part in range(6):
        v = [here[a] for a in ORDERS[part]]
        bases.append((v, (0, v[0] * 256, v[0] * 256 + v[1] * 64)))
    sizes = (256, 64, 16)

    def sem_at(part, stage_no, step):
        return (part * 3 + stage_no) * 3 + step - 1

    def scatter(part, st):
        v, base = bases[part]
        size = sizes[st]
        buf = (r1, r2, r3)[st]
        out = []
        for step in (1, 2, 3):
            rows = pl.ds(pl.multiple_of(base[st] + ((v[st] + step) % 4) * size, size), size)
            i = sem_at(part, st, step)
            out.append(
                send(
                    w.at[part, rows], buf.at[part, step - 1], sel_s.at[i], sel_r.at[i],
                    along(ORDERS[part][st], step),
                )
            )
        return out

    def total(part, st, copies):
        v, base = bases[part]
        size = sizes[st]
        buf = (r1, r2, r3)[st]
        for copy in copies:
            copy.wait()
        start = base[st] + v[st] * size
        span = min(size, 64)

        def chunk(i, carry):
            rows = pl.ds(pl.multiple_of(start + i * span, span), span)
            some = pl.ds(pl.multiple_of(i * span, span), span)
            value = w[part, rows] + buf[part, 0, some] + (buf[part, 1, some] + buf[part, 2, some])
            if st == 2:
                fsl[BLOCK[part], gc, :, pl.ds(part % 2 * WIDE, WIDE)] = value
            else:
                w[part, rows] = value
            return carry

        lax.fori_loop(0, size // span, chunk, 0)

    def gather(slot):
        return [
            send(
                fsl.at[slot, gc], fsl.at[slot, gc], f_s.at[slot * 7 + i], f_r.at[slot * 7 + i],
                (gr, row_peer(i, 1)),
            )
            for i in range(7)
        ]

    def finish(copies):
        for copy in copies:
            copy.wait()

    def target(t, i):
        value = jnp.zeros((128, COLS), F32)
        for j in range(8):
            part = rhs[pl.ds(pl.multiple_of(j * NB + i * 128, 128), 128), :]
            value = jnp.where(flag(t * 8 + j) > 0.5, part, value)
        high = value.astype(BF16)
        return high, (value - high.astype(F32)).astype(BF16)

    def leading():
        def split(i, carry):
            rows = pl.ds(pl.multiple_of(i * 128, 128), 128)
            thl[rows, pl.ds(0, COLS)], thl[rows, pl.ds(COLS, COLS)] = target(0, i)
            return carry

        lax.fori_loop(0, 8, split, 0)

        def solve(i, carry):
            rows = pl.ds(pl.multiple_of(i * 256, 256), 256)
            both = dot(diag[0, rows], thl[...])
            value = both[:, :COLS] + both[:, COLS:]
            a0[rows] = value
            stage[rows] = value.astype(BF16)
            return carry

        lax.fori_loop(0, 4, solve, 0)

    def later_targets(t):
        def split(i, carry):
            for e, term in enumerate(target(t, i)):
                for q in range(4):
                    tst[t * 2 - 2 + e, i, q] = term[q * 32:(q + 1) * 32]
            return carry

        lax.fori_loop(0, 8, split, 0)

    z_rows = [pl.ds(pl.multiple_of(((z + step) % 4) * 128, 128), 128) for step in range(4)]
    piece = pl.ds(pl.multiple_of(core * HALF + z * 128, 128), 128)

    def a_cores():
        return send(stage.at[theirs], a_in, a_s.at[0], a_r.at[0], partner)

    def a_scatter():
        a_half[...] = stage[mine] + a_in[...]
        return [
            send(a_half.at[z_rows[step]], a_z.at[step - 1], a_s.at[step], a_r.at[step], along(2, step))
            for step in (1, 2, 3)
        ]

    def a_cross():
        a_piece[...] = a_half[z_rows[0]] + a_z[0] + (a_z[1] + a_z[2])
        return send(a_piece, a_y, a_s.at[4], a_r.at[4], along(1, 2))

    def a_gather():
        yf[0, gc, piece] = a_piece[...] + a_y[...]
        block_at = yf.at[0, gc, piece]
        return [
            send(block_at, block_at, a_s.at[4 + step], a_r.at[4 + step], along(2, step))
            for step in (1, 2, 3)
        ]

    def a_share():
        block_at = yf.at[0, gc, mine]
        return send(block_at, block_at, a_s.at[8], a_r.at[8], partner)

    my_four = pl.ds(core * 4, 4)

    def t_sems(t, i):
        return t_s.at[t * 5 - 5 + i], t_r.at[t * 5 - 5 + i]

    def terms(t):
        return pl.ds(t * 2 - 2, 2)

    def t_cores(t):
        return send(tst.at[terms(t), pl.ds(other * 4, 4)], t_in.at[terms(t)], *t_sems(t, 0), partner)

    def t_scatter(t):
        for e in (2 * t - 2, 2 * t - 1):
            t_half[e] = tst[e, my_four] + t_in[e]
        return [
            send(
                t_half.at[terms(t), :, (z + step) % 4], t_z.at[step - 1, terms(t)], *t_sems(t, step),
                along(2, step),
            )
            for step in (1, 2, 3)
        ]

    def t_cross(t):
        for e in (2 * t - 2, 2 * t - 1):
            t_piece[e] = t_half[e, :, z] + t_z[0, e] + (t_z[1, e] + t_z[2, e])
        return send(
            t_piece.at[terms(t), pl.ds((1 - y_hi) * 2, 2)], t_y.at[terms(t)], *t_sems(t, 4), along(1, 2)
        )

    def t_own(t):
        value = jnp.zeros((2, 32, COLS), F32)
        for e in (2 * t - 2, 2 * t - 1):
            value = value + (t_piece[e, pl.ds(y_hi * 2, 2)] + t_y[e]).astype(F32)
        return value.reshape(64, COLS)

    def publish(t, which):
        copies = {}
        for i in which:
            rows = mine if i in DIRECT else piece
            block_at = yf.at[t, gc, rows]
            j = t * 7 + i
            copies[i] = send(block_at, block_at, y_s.at[j], y_r.at[j], (gr, row_peer(i, 1)))
        return copies

    def relay(t, copies):
        out = {}
        for i in ACROSS:
            copies[i].wait()
            block_at = yf.at[t, row_peer(i, -1), piece]
            j = (t * 3 + i - 4) * 3 - 1
            out[i] = [
                send(block_at, block_at, z_s.at[j + step], z_r.at[j + step], along(2, step))
                for step in (1, 2, 3)
            ]
        return out

    def arrive(copies, relays, i):
        if i in DIRECT:
            copies[i].wait()
        else:
            finish(relays[i])

    def to_core(t, i):
        block_at = yf.at[t, row_peer(i, -1), mine]
        j = t * 7 + i
        return send(block_at, block_at, fw_s.at[j], fw_r.at[j], partner)

    run = [None] * 6
    load_d[0].wait()
    load_rhs.wait()
    leading()
    a_copy = a_cores()
    load_f[0].wait()
    finish(fin_copies[:2])
    for part in FIRST:
        build(part, 0, 24 if part < 2 else 26)
        run[part] = scatter(part, 0)
    a_copy.wait()
    z_copies = a_scatter()
    later_targets(1)
    t_copy = t_cores(1)
    build(3, 0, 26)
    load_f[1].wait()
    finish(fin_copies[2:])
    for part in (4, 5):
        build(part, 1, 26)
    finish(z_copies)
    a_copy = a_cross()

    for part in FIRST:
        total(part, 0, run[part])
        run[part] = scatter(part, 1)
    for part in SECOND:
        run[part] = scatter(part, 0)
    t_copy.wait()
    t_copies = t_scatter(1)
    a_copy.wait()
    z_copies = a_gather()
    later_targets(2)
    t2_copy = t_cores(2)

    for part in FIRST:
        total(part, 1, run[part])
        run[part] = scatter(part, 2)
    finish(z_copies)
    a_copy = a_share()
    for part in (0, 1):
        total(part, 2, run[part])
    gathers = [gather(0), None, None]
    total(2, 2, run[2])
    finish(t_copies)
    t_copy = t_cross(1)

    for part in SECOND:
        total(part, 0, run[part])
        run[part] = scatter(part, 1)
    t2_copy.wait()
    t_copies = t_scatter(2)

    def product(slot, t):
        low = jnp.concatenate([fsl[slot, (i % 2) * 4 + i // 2] for i in range(4)], axis=0)
        high = jnp.concatenate([fsl[slot, (i % 2) * 4 + i // 2 + 2] for i in range(4)], axis=0)
        value = dot(low, yf[t, gc, pl.ds(0, HALF)]) + dot(high, yf[t, gc, pl.ds(HALF, HALF)])
        return value.astype(BF16).astype(F32)

    def spread(n, value):
        high = value.astype(BF16)
        both = jnp.concatenate([high, (value - high.astype(F32)).astype(BF16)], axis=1)
        for e in range(2):
            g_full[n, core, y_hi, e, z] = both[e * 32:(e + 1) * 32]
        block_at = g_full.at[n, core, y_hi, :, z]
        copies = [
            send(block_at, block_at, g_s.at[n * 7 + i], g_r.at[n * 7 + i], group[i]) for i in range(7)
        ]
        copies.append(send(block_at, block_at, h_s.at[n * 8 + 7], h_r.at[n * 8 + 7], partner))
        return copies

    def share_spread(n, copies):
        shared = [copies[7]]
        for i, (dz, dy) in enumerate(steps):
            copies[i].wait()
            block_at = g_full.at[n, core, (y_hi + dy) % 2, :, (z + 4 - dz) % 4]
            shared.append(send(block_at, block_at, h_s.at[n * 8 + i], h_r.at[n * 8 + i], partner))
        return shared

    def next_y(t):
        right = g_full[t - 1].reshape(NB, 2 * COLS)

        def tile(i, carry):
            rows = pl.ds(pl.multiple_of(i * 256, 256), 256)
            both = dot(diag[t, rows], right)
            value = both[:, :COLS] + both[:, COLS:]
            ysol[t - 1, rows] = value
            yf[t, gc, rows] = value.astype(BF16)
            return carry

        lax.fori_loop(0, 4, tile, 0)

    for part in SECOND:
        total(part, 1, run[part])
        run[part] = scatter(part, 2)
    a_copy.wait()
    t_copy.wait()
    finish(gathers[0])
    s_copies = spread(0, t_own(1) - product(0, 0))
    for part in SECOND:
        total(part, 2, run[part])
    gathers[1:] = [gather(1), gather(2)]
    finish(t_copies)
    t_copy = t_cross(2)
    shared = share_spread(0, s_copies)
    y_copies = [publish(0, range(7)), None, None]
    relays = [None] * 3
    load_d[1].wait()
    load_d[2].wait()
    finish(shared)
    next_y(1)
    t_copy.wait()
    finish(gathers[1])
    second = t_own(2) - product(1, 0)
    finish(gathers[2])
    s_copies = spread(1, second - product(2, 1))
    y_copies[1] = publish(1, range(7))
    relays[0] = relay(0, y_copies[0])
    finish(share_spread(1, s_copies))
    next_y(2)
    y_copies[2] = publish(2, (3, 4, 5, 6, 0, 1, 2))
    relays[1] = relay(1, y_copies[1])

    load_f[2].wait()
    keeps = [flag(28 + t) > 0.5 for t in range(3)]

    def last(col, put):
        def tile(m, inner):
            rows = pl.ds(pl.multiple_of(m * 256, 256), 256)
            value = jnp.zeros((256, COLS), F32)
            for t in range(3):
                change = dot(panel[t, rows], yf[t, col])
                value = value + jnp.where(keeps[t], change, jnp.zeros_like(change))
            put(rows, value.astype(BF16))
            return inner

        lax.fori_loop(0, 4, tile, 0)

    def put_own(rows, value):
        c_in[gc, rows] = value

    c_copies = [None] * 7

    def collect(i):
        out = []
        for t in range(3):
            arrive(y_copies[t], relays[t], i)
            out.append(to_core(t, i))
        return out

    ahead = collect(LAST[0])
    relays[2] = relay(2, y_copies[2])
    for n, i in enumerate(LAST):
        arrived = ahead
        if n < 6:
            ahead = collect(LAST[n + 1])
        finish(arrived)
        to = INVERSE[i]
        col = row_peer(i, -1)

        def put(rows, value, to=to):
            c_out[to, rows] = value

        last(col, put)
        c_copies[to] = send(c_out.at[to], c_in.at[gc], c_s.at[to], c_r.at[to], (gr, col))

    last(gc, put_own)

    def settle(j):
        def tile(m, inner):
            rows = pl.ds(pl.multiple_of(j * NB + m * 256, 256), 256)
            part = pl.ds(pl.multiple_of(m * 256, 256), 256)
            value = rhs[rows, :] - c_in[j, part].astype(F32)
            for t, solved in enumerate((a0[part], ysol[0, part], ysol[1, part])):
                value = jnp.where(flags[pl.ds(t * 8 + j, 1), :] > 0.5, solved, value)
            rhs[rows, :] = value
            return inner

        lax.fori_loop(0, 4, tile, 0)
        rows = pl.ds(pl.multiple_of(j * NB, NB), NB)
        return rows

    stores = []
    rows = settle(gc)
    stores.append(local(rhs.at[rows], out_ref.at[rows], out_sem.at[7]))
    for i in (INVERSE[n] for n in LAST):
        c_copies[i].wait()
        rows = settle(row_peer(i, -1))
        stores.append(local(rhs.at[rows], out_ref.at[rows], out_sem.at[i]))
    finish(stores)


def shards(right_sides, factor_panel, diag_inverse, block_ids, step_blocks):
    dma = pltpu.SemaphoreType.DMA
    vm = pltpu.VMEM
    return pl.pallas_call(
        kernel,
        out_shape=jax.ShapeDtypeStruct((8 * NB, COLS), F32),
        in_specs=[pl.BlockSpec(memory_space=pltpu.SMEM), pl.BlockSpec(memory_space=pltpu.VMEM)]
        + [pl.BlockSpec(memory_space=pl.ANY)] * 3,
        out_specs=pl.BlockSpec(memory_space=pl.ANY),
        scratch_shapes=[
            vm((32, COLS), F32),
            vm((8 * NB, COLS), F32),
            vm((3, NB, NB), BF16),
            vm((3, NB, NB), BF16),
            vm((2, NB, HALF), BF16),
            vm((6, NB, WIDE), BF16),
            vm((3, 8, 16, HALF), BF16),
            vm((6, 3, 256, WIDE), BF16),
            vm((6, 3, 64, WIDE), BF16),
            vm((6, 3, 16, WIDE), BF16),
            vm((NB, 2 * COLS), BF16),
            vm((NB, COLS), F32),
            vm((NB, COLS), BF16),
            vm((HALF, COLS), BF16),
            vm((HALF, COLS), BF16),
            vm((3, 128, COLS), BF16),
            vm((128, COLS), BF16),
            vm((128, COLS), BF16),
            vm((4, 8, 4, 32, COLS), BF16),
            vm((4, 4, 4, 32, COLS), BF16),
            vm((4, 4, 4, 32, COLS), BF16),
            vm((3, 4, 4, 32, COLS), BF16),
            vm((4, 4, 32, COLS), BF16),
            vm((4, 2, 32, COLS), BF16),
            vm((3, 8, NB, COLS), BF16),
            vm((2, NB, COLS), F32),
            vm((2, 2, 2, 2, 4, 32, 2 * COLS), BF16),
            vm((7, NB, COLS), BF16),
            vm((8, NB, COLS), BF16),
            dma((7,)), dma((8,)),
            dma((4,)), dma((4,)),
            dma((54,)), dma((54,)),
            dma((21,)), dma((21,)),
            dma((9,)), dma((9,)),
            dma((10,)), dma((10,)),
            dma((21,)), dma((21,)),
            dma((27,)), dma((27,)),
            dma((21,)), dma((21,)),
            dma((14,)), dma((14,)),
            dma((16,)), dma((16,)),
            dma((7,)), dma((7,)),
        ],
        compiler_params=pltpu.CompilerParams(
            collective_id=0, has_side_effects=True, vmem_limit_bytes=60 << 20
        ),
        name="solve_steps",
    )(step_blocks, block_ids.reshape(1, 128), right_sides, factor_panel, diag_inverse)


def solution(mesh):
    in_specs = (P("gr", "gc"), P(None, ("gr", "gc"), None), P(), P(), P())
    return jax.shard_map(shards, mesh=mesh, in_specs=in_specs, out_specs=P("gr", "gc"), check_vma=False)
```

```python
import jax
import jax.numpy as jnp
from jax import lax
from jax.experimental import pallas as pl
from jax.experimental.pallas import tpu as pltpu
from jax.sharding import PartitionSpec as P

MESH = pl.DeviceIdType.MESH
F32 = jnp.float32
BF16 = jnp.bfloat16
NB = 1024
HALF = 512
COLS = 128
ROW_PEERS = ((2, 0), (1, 0), (3, 0), (0, 1), (2, 1), (1, 1), (3, 1))
DIRECT = ((0, 1, 2, 3), (0, 1, 2, 3), (0, 1, 2, 3))
LAST = (3, 0, 5, 2, 4, 1, 6)
INVERSE = tuple(ROW_PEERS.index(((4 - dx) % 4, flip)) for dx, flip in ROW_PEERS)
ORDERS = ((0, 1, 2), (1, 2, 0), (2, 0, 1)) * 2
BLOCK = (0, 0, 1, 1, 2, 2)
FIRST, SECOND = range(3), range(3, 6)
WIDE = 256


def dot(a, b):
    return jnp.dot(a, b, preferred_element_type=F32)


def kernel(
    steps_ref, ids_ref, rhs_ref, panel_ref, diag_ref, out_ref,
    flags, rhs, panel, diag, fin, w, fsl, r1, r2, r3,
    thl, a0, stage, a_in, a_half, a_z, a_piece, a_y, tst, t_in, t_half, t_z, t_piece, t_y,
    yf, ysol, g_full, c_out, c_in,
    load_sem, out_sem, fin_s, fin_r, sel_s, sel_r, f_s, f_r, a_s, a_r, t_s, t_r,
    y_s, y_r, z_s, z_r, fw_s, fw_r, g_s, g_r, h_s, h_r, c_s, c_r,
):
    gr, gc = lax.axis_index("gr"), lax.axis_index("gc")
    z, y_hi, core = gr // 4, (gr // 2) % 2, gr % 2
    x, y_lo = gc // 2, gc % 2
    y = y_hi * 2 + y_lo
    other = 1 - core
    here = (x, y, z)

    def device(at, c):
        return (at[2] * 4 + (at[1] // 2) * 2 + c, at[0] * 2 + at[1] % 2)

    def along(axis, step):
        at = list(here)
        at[axis] = (at[axis] + step) % 4
        return device(at, core)

    def row_peer(i, sign):
        dx, flip = ROW_PEERS[i]
        return ((x + sign * dx + 4) % 4) * 2 + (y_lo + flip) % 2

    def send(src, dst, s, r, to):
        copy = pltpu.make_async_remote_copy(
            src_ref=src, dst_ref=dst, send_sem=s, recv_sem=r, device_id=to, device_id_type=MESH
        )
        copy.start()
        return copy

    def local(src, dst, sem):
        copy = pltpu.make_async_copy(src, dst, sem)
        copy.start()
        return copy

    partner = (gr + 1 - 2 * core, gc)
    mine = pl.ds(pl.multiple_of(core * HALF, HALF), HALF)
    theirs = pl.ds(pl.multiple_of(other * HALF, HALF), HALF)

    load_d = [local(diag_ref.at[0], diag.at[0], load_sem.at[0])]
    load_rhs = local(rhs_ref, rhs, load_sem.at[1])
    load_f = [local(panel_ref.at[t], panel.at[t], load_sem.at[2 + t]) for t in range(2)]
    load_d += [local(diag_ref.at[t], diag.at[t], load_sem.at[3 + t]) for t in (1, 2)]
    load_f.append(local(panel_ref.at[2], panel.at[2], load_sem.at[6]))

    steps = [(dz, dy) for dz in range(4) for dy in range(2)][1:]
    group = [(((z + dz) % 4) * 4 + ((y_hi + dy) % 2) * 2 + core, gc) for dz, dy in steps]
    peers = group + [(gr, row_peer(i, 1)) for i in range(7)]
    peers += [device((x, (1 - y_hi) * 2 + 1 - y_lo, z), core), partner]
    barrier = pltpu.get_barrier_semaphore()
    for peer in peers:
        pl.semaphore_signal(barrier, inc=1, device_id=peer, device_id_type=MESH)
    pl.semaphore_wait(barrier, len(peers))

    fin_copies = []
    for t in range(2):
        for h in range(2):
            i = t * 2 + h
            fin_copies.append(
                send(
                    panel_ref.at[t, theirs, pl.ds(h * HALF, HALF)],
                    fin.at[t, pl.ds(h * HALF, HALF)],
                    fin_s.at[i], fin_r.at[i], partner,
                )
            )

    lanes = lax.broadcasted_iota(jnp.int32, (1, 128), 1)
    ids = ids_ref[...]
    block = gr * 8 + gc
    beside = (gr + 1 - 2 * core) * 8 + gc
    my_id = jnp.sum(jnp.where(lanes == block, ids.astype(F32), 0.0), axis=1, keepdims=True)
    places = []
    for t in range(3):
        number = steps_ref[t]
        place = jnp.sum(jnp.where(ids == number, lanes.astype(F32), 0.0), axis=1, keepdims=True)
        places.append(jnp.broadcast_to(place, (1, 128)))
        pending = jnp.broadcast_to(my_id, (1, 128)).astype(jnp.int32) > number
        flags[28 + t:29 + t, :] = jnp.where(pending, 1.0, 0.0)
        for j in range(8):
            at = (gr * 8 + j).astype(F32)
            flags[t * 8 + j:t * 8 + j + 1, :] = jnp.where(places[t] == at, 1.0, 0.0)
    for row, t, at in ((24, 1, block), (25, 1, beside), (26, 2, block), (27, 2, beside)):
        flags[row:row + 1, :] = jnp.where(places[t] == at.astype(F32), 1.0, 0.0)

    def flag(row):
        return flags[row:row + 1, :]

    def build(part, t, row):
        col = part % 2 * WIDE

        def mask(r):
            tile = jnp.broadcast_to(flag(r), (128, COLS)).astype(BF16)
            return jnp.concatenate([tile] * (WIDE // COLS), axis=1)

        own, oth = mask(row), mask(row + 1)

        def chunk(i, carry):
            rows = pl.ds(pl.multiple_of(core * HALF + i * 128, 128), 128)
            for h in range(2):
                to = pl.ds(pl.multiple_of(h * HALF + i * 128, 128), 128)
                value = (
                    panel[t, rows, pl.ds(h * HALF + col, WIDE)] * own
                    + fin[t, to, pl.ds(col, WIDE)] * oth
                )
                for m in range(8):
                    at = (m % 2 * 2 + h, i, m // 2)
                    first, second, third = (at[a] for a in ORDERS[part])
                    unit = pl.ds(pl.multiple_of((first * 16 + second * 4 + third) * 16, 16), 16)
                    w[part, unit] = value[m * 16:(m + 1) * 16]
            return carry

        lax.fori_loop(0, 4, chunk, 0)

    bases = []
    for part in range(6):
        v = [here[a] for a in ORDERS[part]]
        bases.append((v, (0, v[0] * 256, v[0] * 256 + v[1] * 64)))
    sizes = (256, 64, 16)

    def sem_at(part, stage_no, step):
        return (part * 3 + stage_no) * 3 + step - 1

    def scatter(part, st):
        v, base = bases[part]
        size = sizes[st]
        buf = (r1, r2, r3)[st]
        out = []
        for step in (1, 2, 3):
            rows = pl.ds(pl.multiple_of(base[st] + ((v[st] + step) % 4) * size, size), size)
            i = sem_at(part, st, step)
            out.append(
                send(
                    w.at[part, rows], buf.at[part, step - 1], sel_s.at[i], sel_r.at[i],
                    along(ORDERS[part][st], step),
                )
            )
        return out

    def total(part, st, copies):
        v, base = bases[part]
        size = sizes[st]
        buf = (r1, r2, r3)[st]
        for copy in copies:
            copy.wait()
        start = base[st] + v[st] * size
        span = min(size, 64)

        def chunk(i, carry):
            rows = pl.ds(pl.multiple_of(start + i * span, span), span)
            some = pl.ds(pl.multiple_of(i * span, span), span)
            value = w[part, rows] + buf[part, 0, some] + (buf[part, 1, some] + buf[part, 2, some])
            if st == 2:
                fsl[BLOCK[part], gc, :, pl.ds(part % 2 * WIDE, WIDE)] = value
            else:
                w[part, rows] = value
            return carry

        lax.fori_loop(0, size // span, chunk, 0)

    def gather(slot):
        return [
            send(
                fsl.at[slot, gc], fsl.at[slot, gc], f_s.at[slot * 7 + i], f_r.at[slot * 7 + i],
                (gr, row_peer(i, 1)),
            )
            for i in range(7)
        ]

    def finish(copies):
        for copy in copies:
            copy.wait()

    def target(t, i):
        value = jnp.zeros((128, COLS), F32)
        for j in range(8):
            part = rhs[pl.ds(pl.multiple_of(j * NB + i * 128, 128), 128), :]
            value = jnp.where(flag(t * 8 + j) > 0.5, part, value)
        high = value.astype(BF16)
        return high, (value - high.astype(F32)).astype(BF16)

    def leading():
        def split(i, carry):
            rows = pl.ds(pl.multiple_of(i * 128, 128), 128)
            thl[rows, pl.ds(0, COLS)], thl[rows, pl.ds(COLS, COLS)] = target(0, i)
            return carry

        lax.fori_loop(0, 8, split, 0)

        def solve(i, carry):
            rows = pl.ds(pl.multiple_of(i * 256, 256), 256)
            both = dot(diag[0, rows], thl[...])
            value = both[:, :COLS] + both[:, COLS:]
            a0[rows] = value
            stage[rows] = value.astype(BF16)
            return carry

        lax.fori_loop(0, 4, solve, 0)

    def later_targets(t):
        def split(i, carry):
            for e, term in enumerate(target(t, i)):
                for q in range(4):
                    tst[t * 2 - 2 + e, i, q] = term[q * 32:(q + 1) * 32]
            return carry

        lax.fori_loop(0, 8, split, 0)

    z_rows = [pl.ds(pl.multiple_of(((z + step) % 4) * 128, 128), 128) for step in range(4)]
    piece = pl.ds(pl.multiple_of(core * HALF + z * 128, 128), 128)

    def a_cores():
        return send(stage.at[theirs], a_in, a_s.at[0], a_r.at[0], partner)

    def a_scatter():
        a_half[...] = stage[mine] + a_in[...]
        return [
            send(a_half.at[z_rows[step]], a_z.at[step - 1], a_s.at[step], a_r.at[step], along(2, step))
            for step in (1, 2, 3)
        ]

    def a_cross():
        a_piece[...] = a_half[z_rows[0]] + a_z[0] + (a_z[1] + a_z[2])
        return send(a_piece, a_y, a_s.at[4], a_r.at[4], along(1, 2))

    def a_gather():
        yf[0, gc, piece] = a_piece[...] + a_y[...]
        block_at = yf.at[0, gc, piece]
        return [
            send(block_at, block_at, a_s.at[4 + step], a_r.at[4 + step], along(2, step))
            for step in (1, 2, 3)
        ]

    def a_share():
        block_at = yf.at[0, gc, mine]
        return send(block_at, block_at, a_s.at[8], a_r.at[8], partner)

    my_four = pl.ds(core * 4, 4)

    def t_sems(t, i):
        return t_s.at[t * 5 - 5 + i], t_r.at[t * 5 - 5 + i]

    def terms(t):
        return pl.ds(t * 2 - 2, 2)

    def t_cores(t):
        return send(tst.at[terms(t), pl.ds(other * 4, 4)], t_in.at[terms(t)], *t_sems(t, 0), partner)

    def t_scatter(t):
        for e in (2 * t - 2, 2 * t - 1):
            t_half[e] = tst[e, my_four] + t_in[e]
        return [
            send(
                t_half.at[terms(t), :, (z + step) % 4], t_z.at[step - 1, terms(t)], *t_sems(t, step),
                along(2, step),
            )
            for step in (1, 2, 3)
        ]

    def t_cross(t):
        for e in (2 * t - 2, 2 * t - 1):
            t_piece[e] = t_half[e, :, z] + t_z[0, e] + (t_z[1, e] + t_z[2, e])
        return send(
            t_piece.at[terms(t), pl.ds((1 - y_hi) * 2, 2)], t_y.at[terms(t)], *t_sems(t, 4), along(1, 2)
        )

    def t_own(t):
        value = jnp.zeros((2, 32, COLS), F32)
        for e in (2 * t - 2, 2 * t - 1):
            value = value + (t_piece[e, pl.ds(y_hi * 2, 2)] + t_y[e]).astype(F32)
        return value.reshape(64, COLS)

    def publish(t, which):
        copies = {}
        for i in which:
            rows = mine if i in DIRECT[t] else piece
            block_at = yf.at[t, gc, rows]
            j = t * 7 + i
            copies[i] = send(block_at, block_at, y_s.at[j], y_r.at[j], (gr, row_peer(i, 1)))
        return copies

    def relay(t, copies):
        out = {}
        for i in LAST:
            if i in DIRECT[t]:
                continue
            copies[i].wait()
            block_at = yf.at[t, row_peer(i, -1), piece]
            j = (t * 7 + i) * 3 - 1
            out[i] = [
                send(block_at, block_at, z_s.at[j + step], z_r.at[j + step], along(2, step))
                for step in (1, 2, 3)
            ]
        return out

    def arrive(t, copies, relays, i):
        if i in DIRECT[t]:
            copies[i].wait()
        else:
            finish(relays[i])

    def to_core(t, i):
        block_at = yf.at[t, row_peer(i, -1), mine]
        j = t * 7 + i
        return send(block_at, block_at, fw_s.at[j], fw_r.at[j], partner)

    run = [None] * 6
    load_d[0].wait()
    load_rhs.wait()
    leading()
    a_copy = a_cores()
    load_f[0].wait()
    finish(fin_copies[:2])
    for part in FIRST:
        build(part, 0, 24 if part < 2 else 26)
        run[part] = scatter(part, 0)
    a_copy.wait()
    z_copies = a_scatter()
    later_targets(1)
    t_copy = t_cores(1)
    build(3, 0, 26)
    load_f[1].wait()
    finish(fin_copies[2:])
    for part in (4, 5):
        build(part, 1, 26)
    finish(z_copies)
    a_copy = a_cross()

    for part in FIRST:
        total(part, 0, run[part])
        run[part] = scatter(part, 1)
    for part in SECOND:
        run[part] = scatter(part, 0)
    t_copy.wait()
    t_copies = t_scatter(1)
    a_copy.wait()
    z_copies = a_gather()
    later_targets(2)
    t2_copy = t_cores(2)

    for part in FIRST:
        total(part, 1, run[part])
        run[part] = scatter(part, 2)
    finish(z_copies)
    a_copy = a_share()
    for part in (0, 1):
        total(part, 2, run[part])
    gathers = [gather(0), None, None]
    total(2, 2, run[2])
    finish(t_copies)
    t_copy = t_cross(1)

    for part in SECOND:
        total(part, 0, run[part])
        run[part] = scatter(part, 1)
    t2_copy.wait()
    t_copies = t_scatter(2)

    def product(slot, t):
        low = jnp.concatenate([fsl[slot, (i % 2) * 4 + i // 2] for i in range(4)], axis=0)
        high = jnp.concatenate([fsl[slot, (i % 2) * 4 + i // 2 + 2] for i in range(4)], axis=0)
        value = dot(low, yf[t, gc, pl.ds(0, HALF)]) + dot(high, yf[t, gc, pl.ds(HALF, HALF)])
        return value.astype(BF16).astype(F32)

    def spread(n, value):
        high = value.astype(BF16)
        both = jnp.concatenate([high, (value - high.astype(F32)).astype(BF16)], axis=1)
        for e in range(2):
            g_full[n, core, y_hi, e, z] = both[e * 32:(e + 1) * 32]
        block_at = g_full.at[n, core, y_hi, :, z]
        copies = [
            send(block_at, block_at, g_s.at[n * 7 + i], g_r.at[n * 7 + i], group[i]) for i in range(7)
        ]
        copies.append(send(block_at, block_at, h_s.at[n * 8 + 7], h_r.at[n * 8 + 7], partner))
        return copies

    def share_spread(n, copies):
        shared = [copies[7]]
        for i, (dz, dy) in enumerate(steps):
            copies[i].wait()
            block_at = g_full.at[n, core, (y_hi + dy) % 2, :, (z + 4 - dz) % 4]
            shared.append(send(block_at, block_at, h_s.at[n * 8 + i], h_r.at[n * 8 + i], partner))
        return shared

    def next_y(t):
        right = g_full[t - 1].reshape(NB, 2 * COLS)

        def tile(i, carry):
            rows = pl.ds(pl.multiple_of(i * 256, 256), 256)
            both = dot(diag[t, rows], right)
            value = both[:, :COLS] + both[:, COLS:]
            ysol[t - 1, rows] = value
            yf[t, gc, rows] = value.astype(BF16)
            return carry

        lax.fori_loop(0, 4, tile, 0)

    for part in SECOND:
        total(part, 1, run[part])
        run[part] = scatter(part, 2)
    a_copy.wait()
    t_copy.wait()
    finish(gathers[0])
    s_copies = spread(0, t_own(1) - product(0, 0))
    for part in SECOND:
        total(part, 2, run[part])
    gathers[1:] = [gather(1), gather(2)]
    finish(t_copies)
    t_copy = t_cross(2)
    shared = share_spread(0, s_copies)
    y_copies = [publish(0, range(7)), None, None]
    relays = [None] * 3
    load_d[1].wait()
    load_d[2].wait()
    finish(shared)
    next_y(1)
    t_copy.wait()
    finish(gathers[1])
    second = t_own(2) - product(1, 0)
    finish(gathers[2])
    s_copies = spread(1, second - product(2, 1))
    y_copies[1] = publish(1, range(7))
    relays[0] = relay(0, y_copies[0])
    finish(share_spread(1, s_copies))
    next_y(2)
    y_copies[2] = publish(2, (3, 0, 4, 5, 6, 1, 2))
    relays[1] = relay(1, y_copies[1])

    load_f[2].wait()
    keeps = [flag(28 + t) > 0.5 for t in range(3)]

    def last(col, put):
        def tile(m, inner):
            rows = pl.ds(pl.multiple_of(m * 256, 256), 256)
            value = jnp.zeros((256, COLS), F32)
            for t in range(3):
                change = dot(panel[t, rows], yf[t, col])
                value = value + jnp.where(keeps[t], change, jnp.zeros_like(change))
            put(rows, value.astype(BF16))
            return inner

        lax.fori_loop(0, 4, tile, 0)

    def put_own(rows, value):
        c_in[gc, rows] = value

    c_copies = [None] * 7

    def collect(i):
        out = []
        for t in range(3):
            arrive(t, y_copies[t], relays[t], i)
            out.append(to_core(t, i))
        return out

    if LAST[0] in DIRECT[2]:
        ahead = collect(LAST[0])
        relays[2] = relay(2, y_copies[2])
    else:
        relays[2] = relay(2, y_copies[2])
        ahead = collect(LAST[0])
    for n, i in enumerate(LAST):
        arrived = ahead
        if n < 6:
            ahead = collect(LAST[n + 1])
        finish(arrived)
        to = INVERSE[i]
        col = row_peer(i, -1)

        def put(rows, value, to=to):
            c_out[to, rows] = value

        last(col, put)
        c_copies[to] = send(c_out.at[to], c_in.at[gc], c_s.at[to], c_r.at[to], (gr, col))

    last(gc, put_own)

    def settle(j):
        def tile(m, inner):
            rows = pl.ds(pl.multiple_of(j * NB + m * 256, 256), 256)
            part = pl.ds(pl.multiple_of(m * 256, 256), 256)
            value = rhs[rows, :] - c_in[j, part].astype(F32)
            for t, solved in enumerate((a0[part], ysol[0, part], ysol[1, part])):
                value = jnp.where(flags[pl.ds(t * 8 + j, 1), :] > 0.5, solved, value)
            rhs[rows, :] = value
            return inner

        lax.fori_loop(0, 4, tile, 0)
        rows = pl.ds(pl.multiple_of(j * NB, NB), NB)
        return rows

    stores = []
    rows = settle(gc)
    stores.append(local(rhs.at[rows], out_ref.at[rows], out_sem.at[7]))
    for i in (INVERSE[n] for n in LAST):
        c_copies[i].wait()
        rows = settle(row_peer(i, -1))
        stores.append(local(rhs.at[rows], out_ref.at[rows], out_sem.at[i]))
    finish(stores)


def shards(right_sides, factor_panel, diag_inverse, block_ids, step_blocks):
    dma = pltpu.SemaphoreType.DMA
    vm = pltpu.VMEM
    return pl.pallas_call(
        kernel,
        out_shape=jax.ShapeDtypeStruct((8 * NB, COLS), F32),
        in_specs=[pl.BlockSpec(memory_space=pltpu.SMEM), pl.BlockSpec(memory_space=pltpu.VMEM)]
        + [pl.BlockSpec(memory_space=pl.ANY)] * 3,
        out_specs=pl.BlockSpec(memory_space=pl.ANY),
        scratch_shapes=[
            vm((32, COLS), F32),
            vm((8 * NB, COLS), F32),
            vm((3, NB, NB), BF16),
            vm((3, NB, NB), BF16),
            vm((2, NB, HALF), BF16),
            vm((6, NB, WIDE), BF16),
            vm((3, 8, 16, HALF), BF16),
            vm((6, 3, 256, WIDE), BF16),
            vm((6, 3, 64, WIDE), BF16),
            vm((6, 3, 16, WIDE), BF16),
            vm((NB, 2 * COLS), BF16),
            vm((NB, COLS), F32),
            vm((NB, COLS), BF16),
            vm((HALF, COLS), BF16),
            vm((HALF, COLS), BF16),
            vm((3, 128, COLS), BF16),
            vm((128, COLS), BF16),
            vm((128, COLS), BF16),
            vm((4, 8, 4, 32, COLS), BF16),
            vm((4, 4, 4, 32, COLS), BF16),
            vm((4, 4, 4, 32, COLS), BF16),
            vm((3, 4, 4, 32, COLS), BF16),
            vm((4, 4, 32, COLS), BF16),
            vm((4, 2, 32, COLS), BF16),
            vm((3, 8, NB, COLS), BF16),
            vm((2, NB, COLS), F32),
            vm((2, 2, 2, 2, 4, 32, 2 * COLS), BF16),
            vm((7, NB, COLS), BF16),
            vm((8, NB, COLS), BF16),
            dma((7,)), dma((8,)),
            dma((4,)), dma((4,)),
            dma((54,)), dma((54,)),
            dma((21,)), dma((21,)),
            dma((9,)), dma((9,)),
            dma((10,)), dma((10,)),
            dma((21,)), dma((21,)),
            dma((63,)), dma((63,)),
            dma((21,)), dma((21,)),
            dma((14,)), dma((14,)),
            dma((16,)), dma((16,)),
            dma((7,)), dma((7,)),
        ],
        compiler_params=pltpu.CompilerParams(
            collective_id=0, has_side_effects=True, vmem_limit_bytes=60 << 20
        ),
        name="solve_steps",
    )(step_blocks, block_ids.reshape(1, 128), right_sides, factor_panel, diag_inverse)


def solution(mesh):
    in_specs = (P("gr", "gc"), P(None, ("gr", "gc"), None), P(), P(), P())
    return jax.shard_map(shards, mesh=mesh, in_specs=in_specs, out_specs=P("gr", "gc"), check_vma=False)
```
